256 devices in a mesh: prow: 32 (over z, x_lo, core), pcol: 8 (over y, x_hi).
Axes of the slice: x: 4 (x_hi: 2, x_lo: 2; x = x_hi * 2 + x_lo), y: 4, z: 8, core: 2. Of those that a mesh axis runs over, the one named last changes fastest.
Arguments:
- panel: bfloat16 [16384, 4096], P('prow', 'pcol'), may hold values from -0.0625 to 0.0625
- anc_inverse: bfloat16 [16384, 16384], P('prow', 'pcol'), may hold values from -6 to 6
- diag_inverse: bfloat16 [4096, 4096], P('prow', 'pcol'), may hold values from -6 to 6
- block_counts: int32 [32], replicated, may hold values from 0 to 4, as said below
Outputs:
- off_diag: bfloat16 [16384, 4096], P('prow', 'pcol')
- diag_block: float32 [4096, 4096], P('prow', 'pcol')
The draws below stay inside these ranges and needn't reach their ends.
Inputs may be any that keep to these rules, and one draw needn't show every extreme that they name: `block_counts`: they add up to exactly 64, and some grid row owns 4 blocks.
All inputs are finite; a program needn't handle non-finite values.
Results may differ from the reference program's by a relative error of at most 0.002.
Values may be sent and summed in bfloat16 or wider, within the bound.
A program may use at most 128 MiB of HBM per device.

```python
import jax
import jax.numpy as jnp
from jax import lax

S = 4096
BLK = 128
BLK_DEV = 2
SLOT_ROWS = 512
ROWS = 8192
SLOTS = 16384
N_PROW = 32


def draw_block_counts(key, part):
    key_order = jax.random.fold_in(key, 11)
    key_amount = jax.random.fold_in(key, 12)
    ordering = jax.random.permutation(key_order, N_PROW)
    half_count = N_PROW // 2
    amounts = jax.random.randint(key_amount, (half_count,), 0, BLK_DEV + 1)
    amounts = amounts.at[0].set(BLK_DEV)
    result_counts = jnp.full((N_PROW,), BLK_DEV, jnp.int32)
    result_counts = result_counts.at[ordering[:half_count]].add(amounts)
    result_counts = result_counts.at[ordering[half_count:2 * half_count]].add(-amounts)
    return result_counts.astype(jnp.int32)


def draw_anc_inverse(key, part):
    key_values = jax.random.fold_in(key, 21)
    values = jnp.clip(jax.random.normal(key_values, (SLOTS, SLOTS), jnp.float32), -4.0, 4.0)
    return ((values + values.T) * 0.70710678).astype(jnp.bfloat16)


def steps_of(rng, extent, split, low, largest):
    def one(position, blocks):
        draws = jax.random.uniform(jax.random.fold_in(jax.random.fold_in(rng, 6), position), (blocks,), jnp.float32, low / len(split), largest / len(split))
        return jnp.repeat(jnp.exp(draws), extent[position] // blocks).reshape((-1,) + (1,) * (len(extent) - position - 1))

    loudness = one(*split[0])
    for cut in split[1:]:
        loudness = loudness * one(*cut)
    return loudness


def scatter_about(own_key, shape, scale, reach, pieces=(), kind=jnp.bfloat16):
    factor_of = steps_of(own_key, shape, pieces, -0.22, 0.18) if pieces else 1.0
    entries = jax.random.normal(own_key, shape, jnp.float32) * scale * factor_of
    return jnp.minimum(jnp.maximum(entries, -reach), reach).astype(kind)


def setup_inputs(seed: int = 0) -> dict:
    key_of = jax.random.split(jax.random.key(seed), 5)
    return {
        "panel": scatter_about(key_of[0], (SLOTS, S), ROWS ** -0.5, 0.0625, ((0, 32), (1, 8))),
        "anc_inverse": draw_anc_inverse(jax.random.fold_in(key_of[4], 71), 0),
        "diag_inverse": scatter_about(key_of[2], (S, S), 1.0, 6.0, ((0, 32), (1, 8))),
        "block_counts": draw_block_counts(jax.random.fold_in(key_of[4], 71), 0),
    }


def reference(panel, anc_inverse, diag_inverse, block_counts):
    slot_row = jnp.arange(SLOTS)
    owners_of = slot_row // SLOT_ROWS
    block_number = (slot_row % SLOT_ROWS) // BLK
    in_use = (block_number < block_counts[owners_of]).astype(jnp.float32)
    masked_panel = panel.astype(jnp.float32) * in_use[:, None]
    inverse_full = anc_inverse.astype(jnp.float32)
    product = jnp.dot(inverse_full, masked_panel, precision=lax.Precision.HIGHEST)
    off_diag = (-(in_use[:, None] * product)).astype(jnp.bfloat16)
    update = jnp.dot(masked_panel.T, off_diag.astype(jnp.float32), precision=lax.Precision.HIGHEST)
    diag_block = diag_inverse.astype(jnp.float32) - update
    return off_diag, diag_block
```

```python
import functools

import jax
import jax.numpy as jnp
from jax import lax
from jax.experimental import pallas as pl
from jax.experimental.pallas import tpu as pltpu
from jax.sharding import PartitionSpec as P

BLK = 128
MESH = pl.DeviceIdType.MESH
BF = jnp.bfloat16
F32 = jnp.float32
LIMIT = 32000.0


def kernel(
    cnt, panel, anc, diag, off, dout,
    PZ, PF, A4, XT, XQ, XR, SQ, SR, HQ, HR, HSQ, HSR, XF, PZT, DQ, DR, pm,
    a_s, a_r, q_s, q_r, t_s, t_r, g_s, g_r, w_s, w_r, x_s, x_r, h_s, h_r, f_s, f_r, d_s, d_r, loc,
):
    p = lax.axis_index("prow")
    c = lax.axis_index("pcol")
    z, q = p // 4, lax.rem(p, 4)
    xlo, core = q // 2, lax.rem(q, 2)
    y, xh = c // 2, lax.rem(c, 2)
    qc = 2 * xlo + (1 - core)
    qx = 2 * (1 - xlo) + core
    qd = 2 * (1 - xlo) + (1 - core)

    def at_z(k):
        return lax.rem(z + k + 8, 8)

    def at_y(k):
        return lax.rem(y + k + 4, 4)

    def dev(zz, qq, yy, hh):
        return (4 * zz + qq, 2 * yy + hh)

    sends = []

    def send(src, dst, ss, rs, to):
        cp = pltpu.make_async_remote_copy(
            src_ref=src, dst_ref=dst, send_sem=ss, recv_sem=rs, device_id=to, device_id_type=MESH
        )
        cp.start()
        sends.append(cp)

    def got(dst, rs):
        pltpu.make_async_copy(dst, dst, rs).wait()

    barrier = pltpu.get_barrier_semaphore()
    greet = [dev(z, k, y, xh) for k in (qc, qx, qd)]
    greet += [dev(at_z(k), q, y, xh) for k in range(1, 8)]
    greet += [dev(z, q, at_y(k), xh) for k in range(1, 4)]
    greet += [dev(z, q, at_y(k), 1 - xh) for k in range(4)]
    for who in greet:
        pl.semaphore_signal(barrier, inc=1, device_id=who, device_id_type=MESH)
    for k in range(8):
        n = lax.rem(c + k, 8)

        @pl.when((z != c) | (n != c))
        def _():
            pl.semaphore_signal(barrier, inc=1, device_id=(4 * c + q, n), device_id_type=MESH)

    count = cnt[p]
    rows = lax.broadcasted_iota(jnp.int32, (512, 512), 0)
    pm[...] = jnp.where(rows < count * BLK, panel[...].astype(F32), 0.0).astype(BF)
    PZ[c, q] = pm[:, pl.ds(pl.multiple_of(q * BLK, BLK), BLK)]

    pl.semaphore_wait(barrier, jnp.where(z == c, 24, 25))

    for i, k in enumerate((qx, qd, qc)):
        send(
            pm.at[:, pl.ds(pl.multiple_of(k * BLK, BLK), BLK)], PZ.at[c, q],
            q_s.at[i], q_r.at[i], dev(z, k, y, xh),
        )
    own_a = pltpu.make_async_copy(anc, A4.at[q], loc.at[0])
    own_a.start()
    for r in range(4):
        part = pl.ds(r * BLK, BLK)
        send(anc.at[part], A4.at[q, part], a_s.at[0, r], a_r.at[0, r], dev(z, qc, y, xh))
        send(anc.at[part], A4.at[q, part], a_s.at[1, r], a_r.at[1, r], dev(z, qx, y, xh))

    for i, k in enumerate((qx, qd, qc)):
        got(PZ.at[c, k], q_r.at[i])

    for k in range(8):
        s = at_z(k + 1)
        part = pl.ds(pl.multiple_of(s * 64, 64), 64)
        src = PZ.at[c, :, part]
        dst = PF.at[y, :, part, pl.ds(pl.multiple_of(xh * BLK, BLK), BLK)]
        if k < 7:
            send(src, dst, t_s.at[k], t_r.at[c], dev(s, q, z // 2, lax.rem(z, 2)))
        else:
            there = pltpu.make_async_remote_copy(
                src_ref=src, dst_ref=dst, send_sem=t_s.at[k], recv_sem=t_r.at[c],
                device_id=dev(s, q, z // 2, lax.rem(z, 2)), device_id_type=MESH,
            )
            here = pltpu.make_async_copy(src, dst, t_r.at[c])

            @pl.when(z != c)
            def _():
                there.start()

            @pl.when(z == c)
            def _():
                here.start()

    send(PZ.at[c], PZ.at[c], w_s.at[0], w_r.at[0], dev(z, q, y, 1 - xh))
    send(PZ.at[c], PZ.at[c], w_s.at[1], w_r.at[1], dev(z, q, at_y(1), xh))
    send(PZ.at[c], PZ.at[c], w_s.at[2], w_r.at[2], dev(z, q, at_y(3), xh))

    def forward_a(r):
        part = pl.ds(r * BLK, BLK)
        got(A4.at[qx, part], a_r.at[1, r])
        send(A4.at[qx, part], A4.at[qx, part], a_s.at[2, r], a_r.at[2, r], dev(z, qc, y, xh))

    mine = pl.ds(pl.multiple_of(z * 64, 64), 64)
    for n in range(8):
        got(PF.at[n // 2, :, mine, pl.ds(BLK * (n % 2), BLK)], t_r.at[n])

    order = [at_y(2), at_y(1), at_y(3), y]
    right, left = dev(at_z(1), q, y, xh), dev(at_z(7), q, y, xh)

    def piece(o, s):
        return PF.at[order[o], :, pl.ds(pl.multiple_of(s * 64, 64), 64), :]

    for t in range(4):
        for o in range(4):
            if t > 0:
                got(piece(o, at_z(-t)), g_r.at[0, t - 1, o])
                got(piece(o, at_z(t)), g_r.at[1, t - 1, o])
            if t < 3 or o < 2:
                src = piece(o, at_z(-t))
                send(src, src, g_s.at[0, t, o], g_r.at[0, t, o], right)
            if t < 3 or o >= 2:
                src = piece(o, at_z(t))
                send(src, src, g_s.at[1, t, o], g_r.at[1, t, o], left)
        forward_a(t)
        if t == 0:
            other = 2 * y + 1 - xh
            got(PZ.at[other], w_r.at[0])
            send(PZ.at[other], PZ.at[other], w_s.at[3], w_r.at[3], dev(z, q, at_y(1), xh))
            send(PZ.at[other], PZ.at[other], w_s.at[4], w_r.at[4], dev(z, q, at_y(3), xh))
        if t == 1:
            down, up = at_y(-1), at_y(1)
            got(PZ.at[2 * down + xh], w_r.at[1])
            got(PZ.at[2 * up + xh], w_r.at[2])
            got(PZ.at[2 * down + 1 - xh], w_r.at[3])
            got(PZ.at[2 * up + 1 - xh], w_r.at[4])
            fd, fu = PZ.at[2 * down], PZ.at[2 * up + 1]
            send(fd, fd, w_s.at[5], w_r.at[5], dev(z, q, at_y(1), xh))
            send(fu, fu, w_s.at[6], w_r.at[6], dev(z, q, at_y(3), xh))
    far = at_y(2)
    got(PZ.at[2 * far], w_r.at[5])
    got(PZ.at[2 * far + 1], w_r.at[6])

    for k in range(8):
        PZT[BLK * k:BLK * (k + 1), :] = PZ[at_z(k + 1)].reshape(2048, BLK).T

    own_a.wait()
    for r in range(4):
        part = pl.ds(r * BLK, BLK)
        got(A4.at[qc, part], a_r.at[0, r])
        got(A4.at[qd, part], a_r.at[2, r])
    for o in range(4):
        far_z = at_z(4)
        got(piece(o, far_z), g_r.at[0 if o < 2 else 1, 3, o])

    def scale_of(top):
        top = jnp.maximum(jnp.max(top, axis=0, keepdims=True), 1e-30)
        return LIMIT / top, top * (1.0 / LIMIT)

    for o in range(4):
        b = PF[order[o]].reshape(2048, 256)

        def tile(i, top, b=b):
            a = A4[i // 2, pl.ds(pl.multiple_of(lax.rem(i, 2) * 256, 256), 256), :]
            d = jnp.dot(a, b, preferred_element_type=F32)
            XT[pl.ds(pl.multiple_of(i * 256, 256), 256), :] = d
            return jnp.maximum(top, jnp.max(jnp.abs(d).reshape(32, 8, 256), axis=0))

        top = lax.fori_loop(0, 8, tile, jnp.zeros((8, 256), F32))
        if o < 3:
            inv, back = scale_of(top)
            SQ[o] = jnp.broadcast_to(back, (8, 256))

            @pl.loop(0, 8)
            def _(i, inv=inv, o=o):
                part = pl.ds(pl.multiple_of(i * 256, 256), 256)
                XQ[o, part, :] = jnp.round(XT[part, :] * inv).astype(jnp.int16)

            to = dev(z, q, order[o], xh)
            send(SQ.at[o], SR.at[o], x_s.at[1, o], x_r.at[1, o], to)
            send(XQ.at[o], XR.at[o], x_s.at[0, o], x_r.at[0, o], to)

    for o in range(3):
        got(SR.at[o], x_r.at[1, o])
        got(XR.at[o], x_r.at[0, o])

    def add_up(i, top):
        part = pl.ds(pl.multiple_of(i * 256, 256), 256)
        s = XT[part, :]
        for o in range(3):
            s += XR[o, part, :].astype(F32) * SR[o, 0:1, :]
        XT[part, :] = s
        return jnp.maximum(top, jnp.max(jnp.abs(s).reshape(32, 8, 256), axis=0))

    top = lax.fori_loop(0, 8, add_up, jnp.zeros((8, 256), F32))
    inv, back = scale_of(top)
    lower = xh == 0
    inv = jnp.where(lower, inv[:, BLK:], inv[:, :BLK])
    back = jnp.where(lower, back[:, BLK:], back[:, :BLK])
    HSQ[...] = jnp.broadcast_to(back, (8, BLK))
    keep = pl.ds(pl.multiple_of(xh * BLK, BLK), BLK)
    give = pl.ds(pl.multiple_of((1 - xh) * BLK, BLK), BLK)

    @pl.loop(0, 8)
    def _(i):
        part = pl.ds(pl.multiple_of(i * 256, 256), 256)
        HQ[part, :] = jnp.round(XT[part, give] * inv).astype(jnp.int16)

    to = dev(z, q, y, 1 - xh)
    send(HSQ, HSR, h_s.at[1], h_r.at[1], to)
    send(HQ, HR, h_s.at[0], h_r.at[0], to)
    got(HSR, h_r.at[1])
    got(HR, h_r.at[0])

    quarter = pl.ds(pl.multiple_of(q * BLK, BLK), BLK)
    slot = lax.broadcasted_iota(jnp.int32, (512, BLK), 0)
    for k in range(4):
        part = pl.ds(512 * k, 512)
        s = XT[part, keep] + HR[part, :].astype(F32) * HSR[0:1, :]
        XF[k, :, quarter] = jnp.where(slot < cnt[4 * z + k] * BLK, -s, 0.0).astype(BF)
        src = XF.at[k, :, quarter]
        send(src, src, f_s.at[0, k], f_r.at[0, k], dev(z, qx, y, xh))
        send(src, src, f_s.at[1, k], f_r.at[1, k], dev(z, qc, y, xh))

    def quart(k, who):
        return XF.at[k, :, pl.ds(pl.multiple_of(who * BLK, BLK), BLK)]

    for k in range(4):
        src = quart(k, qx)
        got(src, f_r.at[0, k])
        send(src, src, f_s.at[2, k], f_r.at[2, k], dev(z, qc, y, xh))
    for k in range(4):
        got(quart(k, qc), f_r.at[1, k])
        got(quart(k, qd), f_r.at[2, k])

    x = XF[...].reshape(2048, 512)
    for t in range(4):
        d = jnp.dot(PZT[256 * t:256 * (t + 1), :], x, preferred_element_type=F32)
        for h in range(2):
            k = 2 * t + h
            if k < 7:
                DQ[k] = d[BLK * h:BLK * (h + 1)].astype(BF)
                send(DQ.at[k], DR.at[k], d_s.at[k], d_r.at[k], dev(at_z(k + 1), q, y, xh))
            else:
                total = d[BLK * h:]
    off[...] = XF[q]
    for k in range(7):
        got(DR.at[k], d_r.at[k])
        total += DR[k].astype(F32)
    dout[...] = diag[...].astype(F32) - total

    for cp in sends:
        cp.wait_send()

    @pl.when(z != c)
    def _():
        there.wait_send()


def per_device(panel, anc_inverse, diag_inverse, block_counts):
    vmem = functools.partial(pl.BlockSpec, memory_space=pltpu.VMEM)
    dma = pltpu.SemaphoreType.DMA
    i16 = jnp.int16
    return pl.pallas_call(
        kernel,
        out_shape=(
            jax.ShapeDtypeStruct((512, 512), BF),
            jax.ShapeDtypeStruct((BLK, 512), F32),
        ),
        in_specs=[pl.BlockSpec(memory_space=pltpu.SMEM), vmem(), vmem(), vmem()],
        out_specs=(vmem(), vmem()),
        scratch_shapes=[
            pltpu.VMEM((8, 4, 512, BLK), BF),
            pltpu.VMEM((4, 4, 512, 256), BF),
            pltpu.VMEM((4, 512, 2048), BF),
            pltpu.VMEM((2048, 256), F32),
            pltpu.VMEM((3, 2048, 256), i16),
            pltpu.VMEM((3, 2048, 256), i16),
            pltpu.VMEM((3, 8, 256), F32),
            pltpu.VMEM((3, 8, 256), F32),
            pltpu.VMEM((2048, BLK), i16),
            pltpu.VMEM((2048, BLK), i16),
            pltpu.VMEM((8, BLK), F32),
            pltpu.VMEM((8, BLK), F32),
            pltpu.VMEM((4, 512, 512), BF),
            pltpu.VMEM((1024, 2048), BF),
            pltpu.VMEM((7, BLK, 512), BF),
            pltpu.VMEM((7, BLK, 512), BF),
            pltpu.VMEM((512, 512), BF),
            dma((3, 4)), dma((3, 4)), dma((3,)), dma((3,)), dma((8,)), dma((8,)),
            dma((2, 4, 4)), dma((2, 4, 4)), dma((7,)), dma((7,)), dma((2, 3)), dma((2, 3)),
            dma((2,)), dma((2,)), dma((3, 4)), dma((3, 4)), dma((7,)), dma((7,)), dma((1,)),
        ],
        compiler_params=pltpu.CompilerParams(
            collective_id=0, has_side_effects=True, vmem_limit_bytes=56 << 20
        ),
        cost_estimate=pl.CostEstimate(
            flops=10_737_418_240, bytes_accessed=4 << 20, transcendentals=0
        ),
        name="selected_inversion",
    )(block_counts, panel, anc_inverse, diag_inverse)


def solution(mesh):
    return jax.shard_map(
        per_device,
        mesh=mesh,
        in_specs=(P("prow", "pcol"), P("prow", "pcol"), P("prow", "pcol"), P()),
        out_specs=(P("prow", "pcol"), P("prow", "pcol")),
        check_vma=False,
    )
```

```python
import functools

import jax
import jax.numpy as jnp
from jax import lax
from jax.experimental import pallas as pl
from jax.experimental.pallas import tpu as pltpu
from jax.sharding import PartitionSpec as P

BLK = 128
MESH = pl.DeviceIdType.MESH
BF = jnp.bfloat16
F32 = jnp.float32
LIMIT = 32000.0
EARLY = 1


def kernel(
    cnt, panel, anc, diag, off, dout,
    PZ, PF, A4, XT, TMP, DT, XQ, XR, SQ, SR, GQ, GR, GSQ, GSR, XK, YQ, YR, YSQ, YSR, HQ, HR, HSQ, HSR, XF, PZT, DQ, DR, pm,
    a_s, a_r, q_s, q_r, t_s, t_r, g_s, g_r, w_s, w_r, x_s, x_r, b_s, b_r, h_s, h_r, f_s, f_r, d_s, d_r, loc,
):
    p = lax.axis_index("prow")
    c = lax.axis_index("pcol")
    z, q = p // 4, lax.rem(p, 4)
    xlo, core = q // 2, lax.rem(q, 2)
    y, xh = c // 2, lax.rem(c, 2)
    qc = 2 * xlo + (1 - core)
    qx = 2 * (1 - xlo) + core
    qd = 2 * (1 - xlo) + (1 - core)

    def at_z(k):
        return lax.rem(z + k + 8, 8)

    def at_y(k):
        return lax.rem(y + k + 4, 4)

    def dev(zz, qq, yy, hh):
        return (4 * zz + qq, 2 * yy + hh)

    sends = []

    def send(src, dst, ss, rs, to):
        cp = pltpu.make_async_remote_copy(
            src_ref=src, dst_ref=dst, send_sem=ss, recv_sem=rs, device_id=to, device_id_type=MESH
        )
        cp.start()
        sends.append(cp)

    def got(dst, rs):
        pltpu.make_async_copy(dst, dst, rs).wait()

    barrier = pltpu.get_barrier_semaphore()
    greet = [(4 * c + q, lax.rem(c + k, 8)) for k in range(1, 8)]
    greet += [dev(at_z(k), q, y, xh) for k in (4, 3, 5, 2, 6, 1, 7)]
    greet += [dev(z, q, at_y(k), xh) for k in (2, 1, 3)]
    greet += [dev(z, q, y, 1 - xh)]
    greet += [dev(z, k, y, xh) for k in (qd, qx, qc)]
    for who in greet:
        pl.semaphore_signal(barrier, inc=1, device_id=who, device_id_type=MESH)

    count = cnt[p]
    rows = lax.broadcasted_iota(jnp.int32, (512, 512), 0)
    pm[...] = jnp.where(rows < count * BLK, panel[...].astype(F32), 0.0).astype(BF)
    PZ[c, q] = pm[:, pl.ds(pl.multiple_of(q * BLK, BLK), BLK)]

    pl.semaphore_wait(barrier, jnp.where(z == c, 14, 22))

    for i, k in enumerate((qx, qd, qc)):
        send(
            pm.at[:, pl.ds(pl.multiple_of(k * BLK, BLK), BLK)], PZ.at[c, q],
            q_s.at[i], q_r.at[i], dev(z, k, y, xh),
        )
    own_a = pltpu.make_async_copy(anc, A4.at[q], loc.at[0])
    own_a.start()

    def send_a(r):
        part = pl.ds(r * BLK, BLK)
        send(anc.at[part], A4.at[q, part], a_s.at[1, r], a_r.at[1, r], dev(z, qx, y, xh))
        send(anc.at[part], A4.at[q, part], a_s.at[0, r], a_r.at[0, r], dev(z, qc, y, xh))

    def forward_a(r):
        part = pl.ds(r * BLK, BLK)
        got(A4.at[qx, part], a_r.at[1, r])
        send(A4.at[qx, part], A4.at[qx, part], a_s.at[2, r], a_r.at[2, r], dev(z, qc, y, xh))

    for r in range(EARLY):
        send_a(r)
    for i, k in enumerate((qx, qd, qc)):
        got(PZ.at[c, k], q_r.at[i])

    for k in range(8):
        s = at_z(k + 1)
        part = pl.ds(pl.multiple_of(s * 64, 64), 64)
        src = PZ.at[c, :, part]
        dst = PF.at[y, :, part, pl.ds(pl.multiple_of(xh * BLK, BLK), BLK)]
        if k < 7:
            send(src, dst, t_s.at[k], t_r.at[c], dev(s, q, z // 2, lax.rem(z, 2)))
        else:
            there = pltpu.make_async_remote_copy(
                src_ref=src, dst_ref=dst, send_sem=t_s.at[k], recv_sem=t_r.at[c],
                device_id=dev(s, q, z // 2, lax.rem(z, 2)), device_id_type=MESH,
            )
            here = pltpu.make_async_copy(src, dst, t_r.at[c])

            @pl.when(z != c)
            def _():
                there.start()

            @pl.when(z == c)
            def _():
                here.start()

    def rows_over(stage):
        up_to, down_to = dev(z, q, at_y(1), xh), dev(z, q, at_y(3), xh)
        if stage == 0:
            send(PZ.at[c], PZ.at[c], w_s.at[1], w_r.at[1], up_to)
            send(PZ.at[c], PZ.at[c], w_s.at[2], w_r.at[2], down_to)
            send(PZ.at[c], PZ.at[c], w_s.at[0], w_r.at[0], dev(z, q, y, 1 - xh))
        if stage == 1:
            other = 2 * y + 1 - xh
            got(PZ.at[other], w_r.at[0])
            send(PZ.at[other], PZ.at[other], w_s.at[3], w_r.at[3], up_to)
            send(PZ.at[other], PZ.at[other], w_s.at[4], w_r.at[4], down_to)
        if stage == 2:
            down, up = at_y(-1), at_y(1)
            got(PZ.at[2 * down + xh], w_r.at[1])
            got(PZ.at[2 * up + xh], w_r.at[2])
            got(PZ.at[2 * down + 1 - xh], w_r.at[3])
            got(PZ.at[2 * up + 1 - xh], w_r.at[4])
            fd, fu = PZ.at[2 * down], PZ.at[2 * up + 1]
            send(fd, fd, w_s.at[5], w_r.at[5], up_to)
            send(fu, fu, w_s.at[6], w_r.at[6], down_to)
        if stage == 3:
            far = at_y(2)
            got(PZ.at[2 * far], w_r.at[5])
            got(PZ.at[2 * far + 1], w_r.at[6])
            for k in range(8):
                PZT[BLK * k:BLK * (k + 1), :] = PZ[at_z(k + 1)].reshape(2048, BLK).T

    order = [at_y(2), at_y(1), at_y(3), y]
    right, left = dev(at_z(1), q, y, xh), dev(at_z(7), q, y, xh)
    mine = pl.ds(pl.multiple_of(z * 64, 64), 64)

    def piece(o, s):
        return PF.at[order[o], :, pl.ds(pl.multiple_of(s * 64, 64), 64), :]

    def gather_step(o, t):
        if t == 0:
            for h in range(2):
                got(PF.at[order[o], :, mine, pl.ds(BLK * h, BLK)], t_r.at[2 * order[o] + h])
        elif t < 4:
            got(piece(o, at_z(-t)), g_r.at[0, t - 1, o])
            got(piece(o, at_z(t)), g_r.at[1, t - 1, o])
        else:
            got(piece(o, at_z(4)), g_r.at[0 if o < 2 else 1, 3, o])
        if t < 3 or (t == 3 and o < 2):
            src = piece(o, at_z(-t))
            send(src, src, g_s.at[0, t, o], g_r.at[0, t, o], right)
        if t < 3 or (t == 3 and o >= 2):
            src = piece(o, at_z(t))
            send(src, src, g_s.at[1, t, o], g_r.at[1, t, o], left)

    def scale_of(top):
        top = jnp.maximum(jnp.max(top, axis=0, keepdims=True), 1e-30)
        return LIMIT / top, top * (1.0 / LIMIT)

    def first(half):
        return xlo if half == 0 else 1 - xlo

    def half_rows(half):
        return pl.ds(pl.multiple_of(1024 * first(half), 1024), 1024)

    def product(o, half):
        b = PF[order[o]].reshape(2048, 256)

        def tile(i, top):
            a = A4[2 * first(half) + i // 2, pl.ds(pl.multiple_of(lax.rem(i, 2) * 256, 256), 256), :]
            d = jnp.dot(a, b, preferred_element_type=F32)
            if o < 3:
                TMP[pl.ds(pl.multiple_of(i * 256, 256), 256), :] = d
                return jnp.maximum(top, jnp.max(jnp.abs(d).reshape(32, 8, 256), axis=0))
            XT[pl.ds(pl.multiple_of(1024 * first(half) + i * 256, 256), 256), :] = d
            return top

        top = lax.fori_loop(0, 4, tile, jnp.zeros((8, 256), F32))
        if o < 3:
            inv, back = scale_of(top)
            SQ[o, half] = jnp.broadcast_to(back, (8, 256))

            @pl.loop(0, 4)
            def _(i):
                src = pl.ds(pl.multiple_of(i * 256, 256), 256)
                dst = pl.ds(pl.multiple_of(1024 * first(half) + i * 256, 256), 256)
                XQ[o, dst, :] = jnp.round(TMP[src, :] * inv).astype(jnp.int16)

            to = dev(z, q, order[o], xh)
            part = half_rows(half)
            send(SQ.at[o, half], SR.at[o, half], x_s.at[1, o, half], x_r.at[1, o, half], to)
            send(XQ.at[o, part], XR.at[o, part], x_s.at[0, o, half], x_r.at[0, o, half], to)

    def pair_product(o):
        b = PF[order[o]].reshape(2048, 256)

        def tile(i, top):
            a = A4[2 * first(1) + i // 2, pl.ds(pl.multiple_of(lax.rem(i, 2) * 256, 256), 256), :]
            d = jnp.dot(a, b, preferred_element_type=F32)
            TMP[pl.ds(pl.multiple_of(i * 256, 256), 256), :] = d
            return jnp.maximum(top, jnp.max(jnp.abs(d).reshape(32, 8, 256), axis=0))

        top = lax.fori_loop(0, 4, tile, jnp.zeros((8, 256), F32))
        inv, back = scale_of(top)
        inv = jnp.where(xh == 0, inv[:, BLK:], inv[:, :BLK])
        back = jnp.where(xh == 0, back[:, BLK:], back[:, :BLK])
        GSQ[o] = jnp.broadcast_to(back, (8, BLK))

        @pl.loop(0, 4)
        def _(i):
            part = pl.ds(pl.multiple_of(i * 256, 256), 256)
            GQ[o, part, :] = jnp.round(TMP[part, give] * inv).astype(jnp.int16)
            XK[o, part, :] = TMP[part, keep]

        to = dev(z, q, y, 1 - xh)
        send(GSQ.at[o], GSR.at[o], b_s.at[1, o], b_r.at[1, o], to)
        send(GQ.at[o], GR.at[o], b_s.at[0, o], b_r.at[0, o], to)

    def pair_sum(o):
        got(GSR.at[o], b_r.at[1, o])
        got(GR.at[o], b_r.at[0, o])
        scale = GSR[o, 0:1, :]

        def tile(i, top):
            part = pl.ds(pl.multiple_of(i * 256, 256), 256)
            s = XK[o, part, :] + GR[o, part, :].astype(F32) * scale
            XK[o, part, :] = s
            return jnp.maximum(top, jnp.max(jnp.abs(s).reshape(32, 8, BLK), axis=0))

        top = lax.fori_loop(0, 4, tile, jnp.zeros((8, BLK), F32))
        if o < 3:
            inv, back = scale_of(top)
            YSQ[o] = jnp.broadcast_to(back, (8, BLK))

            @pl.loop(0, 4)
            def _(i):
                part = pl.ds(pl.multiple_of(i * 256, 256), 256)
                YQ[o, part, :] = jnp.round(XK[o, part, :] * inv).astype(jnp.int16)

            to = dev(z, q, order[o], xh)
            send(YSQ.at[o], YSR.at[o], x_s.at[1, o, 1], x_r.at[1, o, 1], to)
            send(YQ.at[o], YR.at[o], x_s.at[0, o, 1], x_r.at[0, o, 1], to)

    keep = pl.ds(pl.multiple_of(xh * BLK, BLK), BLK)
    give = pl.ds(pl.multiple_of((1 - xh) * BLK, BLK), BLK)

    def add_up(half):
        rows_here = half_rows(half)
        for o in range(3):
            got(SR.at[o, half], x_r.at[1, o, half])
            got(XR.at[o, rows_here], x_r.at[0, o, half])

        def tile(i, top):
            part = pl.ds(pl.multiple_of(1024 * first(half) + i * 256, 256), 256)
            s = XT[part, :]
            for o in range(3):
                s += XR[o, part, :].astype(F32) * SR[o, half, 0:1, :]
            XT[part, :] = s
            return jnp.maximum(top, jnp.max(jnp.abs(s).reshape(32, 8, 256), axis=0))

        top = lax.fori_loop(0, 4, tile, jnp.zeros((8, 256), F32))
        inv, back = scale_of(top)
        inv = jnp.where(xh == 0, inv[:, BLK:], inv[:, :BLK])
        back = jnp.where(xh == 0, back[:, BLK:], back[:, :BLK])
        HSQ[half] = jnp.broadcast_to(back, (8, BLK))

        @pl.loop(0, 4)
        def _(i):
            part = pl.ds(pl.multiple_of(1024 * first(half) + i * 256, 256), 256)
            HQ[part, :] = jnp.round(XT[part, give] * inv).astype(jnp.int16)

        to = dev(z, q, y, 1 - xh)
        send(HSQ.at[half], HSR.at[half], h_s.at[1, half], h_r.at[1, half], to)
        send(HQ.at[rows_here], HR.at[rows_here], h_s.at[0, half], h_r.at[0, half], to)

    def quart(k, who):
        return XF.at[k, :, pl.ds(pl.multiple_of(who * BLK, BLK), BLK)]

    slot = lax.broadcasted_iota(jnp.int32, (512, BLK), 0)

    def finish_x(half):
        if half == 0:
            got(HSR.at[half], h_r.at[1, half])
            got(HR.at[half_rows(half)], h_r.at[0, half])
        else:
            for o in range(3):
                got(YSR.at[o], x_r.at[1, o, 1])
                got(YR.at[o], x_r.at[0, o, 1])
        for i in range(2):
            k = 2 * first(half) + i
            part = pl.ds(pl.multiple_of(512 * k, 512), 512)
            if half == 0:
                s = XT[part, keep] + HR[part, :].astype(F32) * HSR[half, 0:1, :]
            else:
                here = slice(512 * i, 512 * (i + 1))
                s = XK[3, here, :]
                for o in range(3):
                    s += YR[o, here, :].astype(F32) * YSR[o, 0:1, :]
            XF[k, :, pl.ds(pl.multiple_of(q * BLK, BLK), BLK)] = jnp.where(
                slot < cnt[4 * z + k] * BLK, -s, 0.0
            ).astype(BF)
            src = quart(k, q)
            send(src, src, f_s.at[0, half, i], f_r.at[0, half, i], dev(z, qx, y, xh))
            send(src, src, f_s.at[1, half, i], f_r.at[1, half, i], dev(z, qc, y, xh))

    def pass_x(half):
        for i in range(2):
            src = quart(2 * first(1 - half) + i, qx)
            got(src, f_r.at[0, half, i])
            send(src, src, f_s.at[2, half, i], f_r.at[2, half, i], dev(z, qc, y, xh))

    def diagonal(half):
        cols = pl.ds(pl.multiple_of(256 * first(half), 256), 256)
        x = XF[:, :, cols].reshape(2048, 256)
        for t in range(4):
            d = jnp.dot(PZT[256 * t:256 * (t + 1), :], x, preferred_element_type=F32)
            for h in range(2):
                k = 2 * t + h
                if k < 7:
                    DQ[k, :, cols] = d[BLK * h:BLK * (h + 1)].astype(BF)
                    src, dst = DQ.at[k, :, cols], DR.at[k, :, cols]
                    send(src, dst, d_s.at[half, k], d_r.at[half, k], dev(at_z(k + 1), q, y, xh))
                else:
                    DT[:, cols] = d[BLK * h:]

    rows_over(0)
    for r in range(EARLY, 4):
        send_a(r)

    for w in range(11):
        for o in range(4):
            if 0 <= w - 2 * o <= 4:
                gather_step(o, w - 2 * o)
        if w == 1:
            rows_over(1)
            forward_a(0)
        if w == 3:
            rows_over(2)
            forward_a(1)
        if w == 4:
            own_a.wait()
            for r in range(4):
                got(A4.at[qc, pl.ds(r * BLK, BLK)], a_r.at[0, r])
            product(0, 0)
        if w == 5:
            forward_a(2)
        if w == 6:
            product(1, 0)
        if w == 7:
            forward_a(3)
        if w == 8:
            product(2, 0)
            for r in range(4):
                got(A4.at[qd, pl.ds(r * BLK, BLK)], a_r.at[2, r])
            pair_product(0)
        if w == 9:
            pair_product(1)
    pair_product(2)
    pair_sum(0)
    pair_product(3)
    pair_sum(1)
    product(3, 0)
    pair_sum(2)
    rows_over(3)
    add_up(0)
    pair_sum(3)
    finish_x(0)
    finish_x(1)
    pass_x(0)
    pass_x(1)
    for half in range(2):
        for i in range(2):
            got(quart(2 * first(half) + i, qc), f_r.at[1, half, i])
    diagonal(0)
    for half in range(2):
        for i in range(2):
            got(quart(2 * first(1 - half) + i, qd), f_r.at[2, half, i])
    diagonal(1)
    off[...] = XF[q]
    total = DT[...]
    for k in range(7):
        for half in range(2):
            cols = pl.ds(pl.multiple_of(256 * first(half), 256), 256)
            got(DR.at[k, :, cols], d_r.at[half, k])
        total += DR[k].astype(F32)
    dout[...] = diag[...].astype(F32) - total

    for cp in sends:
        cp.wait_send()

    @pl.when(z != c)
    def _():
        there.wait_send()


def per_device(panel, anc_inverse, diag_inverse, block_counts):
    vmem = functools.partial(pl.BlockSpec, memory_space=pltpu.VMEM)
    dma = pltpu.SemaphoreType.DMA
    i16 = jnp.int16
    return pl.pallas_call(
        kernel,
        out_shape=(
            jax.ShapeDtypeStruct((512, 512), BF),
            jax.ShapeDtypeStruct((BLK, 512), F32),
        ),
        in_specs=[pl.BlockSpec(memory_space=pltpu.SMEM), vmem(), vmem(), vmem()],
        out_specs=(vmem(), vmem()),
        scratch_shapes=[
            pltpu.VMEM((8, 4, 512, BLK), BF),
            pltpu.VMEM((4, 4, 512, 256), BF),
            pltpu.VMEM((4, 512, 2048), BF),
            pltpu.VMEM((2048, 256), F32),
            pltpu.VMEM((1024, 256), F32),
            pltpu.VMEM((BLK, 512), F32),
            pltpu.VMEM((3, 2048, 256), i16),
            pltpu.VMEM((3, 2048, 256), i16),
            pltpu.VMEM((3, 2, 8, 256), F32),
            pltpu.VMEM((3, 2, 8, 256), F32),
            pltpu.VMEM((4, 1024, BLK), i16),
            pltpu.VMEM((4, 1024, BLK), i16),
            pltpu.VMEM((4, 8, BLK), F32),
            pltpu.VMEM((4, 8, BLK), F32),
            pltpu.VMEM((4, 1024, BLK), F32),
            pltpu.VMEM((3, 1024, BLK), i16),
            pltpu.VMEM((3, 1024, BLK), i16),
            pltpu.VMEM((3, 8, BLK), F32),
            pltpu.VMEM((3, 8, BLK), F32),
            pltpu.VMEM((2048, BLK), i16),
            pltpu.VMEM((2048, BLK), i16),
            pltpu.VMEM((2, 8, BLK), F32),
            pltpu.VMEM((2, 8, BLK), F32),
            pltpu.VMEM((4, 512, 512), BF),
            pltpu.VMEM((1024, 2048), BF),
            pltpu.VMEM((7, BLK, 512), BF),
            pltpu.VMEM((7, BLK, 512), BF),
            pltpu.VMEM((512, 512), BF),
            dma((3, 4)), dma((3, 4)), dma((3,)), dma((3,)), dma((8,)), dma((8,)),
            dma((2, 4, 4)), dma((2, 4, 4)), dma((7,)), dma((7,)), dma((2, 3, 2)), dma((2, 3, 2)), dma((2, 4)), dma((2, 4)),
            dma((2, 2)), dma((2, 2)), dma((3, 2, 2)), dma((3, 2, 2)), dma((2, 7)), dma((2, 7)), dma((1,)),
        ],
        compiler_params=pltpu.CompilerParams(
            collective_id=0, has_side_effects=True, vmem_limit_bytes=56 << 20
        ),
        cost_estimate=pl.CostEstimate(
            flops=10_737_418_240, bytes_accessed=4 << 20, transcendentals=0
        ),
        name="selected_inversion",
    )(block_counts, panel, anc_inverse, diag_inverse)


def solution(mesh):
    return jax.shard_map(
        per_device,
        mesh=mesh,
        in_specs=(P("prow", "pcol"), P("prow", "pcol"), P("prow", "pcol"), P()),
        out_specs=(P("prow", "pcol"), P("prow", "pcol")),
        check_vma=False,
    )
```

```python
import functools

import jax
import jax.numpy as jnp
from jax import lax
from jax.experimental import pallas as pl
from jax.experimental.pallas import tpu as pltpu
from jax.sharding import PartitionSpec as P

BLK = 128
MESH = pl.DeviceIdType.MESH
BF = jnp.bfloat16
F32 = jnp.float32
LIMIT = 32000.0
EARLY = 0


def kernel(
    cnt, panel, anc, diag, off, dout,
    PZ, PF, A4, XT, TMP, DP, XQ, XR, SQ, SR, GQ, GR, GSQ, GSR, XK, YQ, YR, YSQ, YSR, HQ, HR, HSQ, HSR, XF, PZT, DQ, DR, DSQ, DSR, pm,
    a_s, a_r, q_s, q_r, t_s, t_r, g_s, g_r, w_s, w_r, x_s, x_r, b_s, b_r, h_s, h_r, f_s, f_r, d_s, d_r, loc,
):
    p = lax.axis_index("prow")
    c = lax.axis_index("pcol")
    z, q = p // 4, lax.rem(p, 4)
    xlo, core = q // 2, lax.rem(q, 2)
    y, xh = c // 2, lax.rem(c, 2)
    qc = 2 * xlo + (1 - core)
    qx = 2 * (1 - xlo) + core
    qd = 2 * (1 - xlo) + (1 - core)

    def at_z(k):
        return lax.rem(z + k + 8, 8)

    def at_y(k):
        return lax.rem(y + k + 4, 4)

    def dev(zz, qq, yy, hh):
        return (4 * zz + qq, 2 * yy + hh)

    sends = []

    def send(src, dst, ss, rs, to):
        cp = pltpu.make_async_remote_copy(
            src_ref=src, dst_ref=dst, send_sem=ss, recv_sem=rs, device_id=to, device_id_type=MESH
        )
        cp.start()
        sends.append(cp)

    def got(dst, rs):
        pltpu.make_async_copy(dst, dst, rs).wait()

    barrier = pltpu.get_barrier_semaphore()
    greet = [(4 * c + q, lax.rem(c + k, 8)) for k in range(1, 8)]
    greet += [dev(at_z(k), q, y, xh) for k in (1, 7)]
    greet += [dev(z, q, at_y(k), xh) for k in (2, 1, 3)]
    greet += [dev(z, q, y, 1 - xh)]
    greet += [dev(z, k, y, xh) for k in (qd, qx, qc)]
    for who in greet:
        pl.semaphore_signal(barrier, inc=1, device_id=who, device_id_type=MESH)

    @pl.when(z != c)
    def _():
        pl.semaphore_signal(barrier, inc=1, device_id=(4 * c + q, c), device_id_type=MESH)

    count = cnt[p]
    rows = lax.broadcasted_iota(jnp.int32, (512, 512), 0)
    pm[...] = jnp.where(rows < count * BLK, panel[...].astype(F32), 0.0).astype(BF)
    PZ[c, q] = pm[:, pl.ds(pl.multiple_of(q * BLK, BLK), BLK)]

    pl.semaphore_wait(barrier, jnp.where(z == c, 16, 17))

    for i, k in enumerate((qx, qd, qc)):
        send(
            pm.at[:, pl.ds(pl.multiple_of(k * BLK, BLK), BLK)], PZ.at[c, q],
            q_s.at[i], q_r.at[i], dev(z, k, y, xh),
        )
    own_a = pltpu.make_async_copy(anc, A4.at[q], loc.at[0])
    own_a.start()

    def send_a(r):
        part = pl.ds(r * BLK, BLK)
        send(anc.at[part], A4.at[q, part], a_s.at[1, r], a_r.at[1, r], dev(z, qx, y, xh))
        send(anc.at[part], A4.at[q, part], a_s.at[0, r], a_r.at[0, r], dev(z, qc, y, xh))

    def forward_a(r):
        part = pl.ds(r * BLK, BLK)
        got(A4.at[qx, part], a_r.at[1, r])
        send(A4.at[qx, part], A4.at[qx, part], a_s.at[2, r], a_r.at[2, r], dev(z, qc, y, xh))

    for r in range(EARLY):
        send_a(r)
    for i, k in enumerate((qx, qd, qc)):
        got(PZ.at[c, k], q_r.at[i])

    for k in range(8):
        s = at_z(k + 1)
        part = pl.ds(pl.multiple_of(s * 64, 64), 64)
        src = PZ.at[c, :, part]
        dst = PF.at[y, :, part, pl.ds(pl.multiple_of(xh * BLK, BLK), BLK)]
        if k < 7:
            send(src, dst, t_s.at[k], t_r.at[c], dev(s, q, z // 2, lax.rem(z, 2)))
        else:
            there = pltpu.make_async_remote_copy(
                src_ref=src, dst_ref=dst, send_sem=t_s.at[k], recv_sem=t_r.at[c],
                device_id=dev(s, q, z // 2, lax.rem(z, 2)), device_id_type=MESH,
            )
            here = pltpu.make_async_copy(src, dst, t_r.at[c])

            @pl.when(z != c)
            def _():
                there.start()

            @pl.when(z == c)
            def _():
                here.start()

    def rows_over(stage):
        up_to, down_to = dev(z, q, at_y(1), xh), dev(z, q, at_y(3), xh)
        if stage == 0:
            send(PZ.at[c], PZ.at[c], w_s.at[1], w_r.at[1], up_to)
            send(PZ.at[c], PZ.at[c], w_s.at[2], w_r.at[2], down_to)
            send(PZ.at[c], PZ.at[c], w_s.at[0], w_r.at[0], dev(z, q, y, 1 - xh))
        if stage == 1:
            other = 2 * y + 1 - xh
            got(PZ.at[other], w_r.at[0])
            send(PZ.at[other], PZ.at[other], w_s.at[3], w_r.at[3], up_to)
            send(PZ.at[other], PZ.at[other], w_s.at[4], w_r.at[4], down_to)
        if stage == 2:
            down, up = at_y(-1), at_y(1)
            got(PZ.at[2 * down + xh], w_r.at[1])
            got(PZ.at[2 * up + xh], w_r.at[2])
            got(PZ.at[2 * down + 1 - xh], w_r.at[3])
            got(PZ.at[2 * up + 1 - xh], w_r.at[4])
            fd, fu = PZ.at[2 * down], PZ.at[2 * up + 1]
            send(fd, fd, w_s.at[5], w_r.at[5], up_to)
            send(fu, fu, w_s.at[6], w_r.at[6], down_to)
        if stage == 3:
            far = at_y(2)
            got(PZ.at[2 * far], w_r.at[5])
            got(PZ.at[2 * far + 1], w_r.at[6])
            for k in range(8):
                PZT[BLK * k:BLK * (k + 1), :] = PZ[at_z(k + 1)].reshape(2048, BLK).T

    order = [at_y(2), at_y(1), at_y(3), y]
    right, left = dev(at_z(1), q, y, xh), dev(at_z(7), q, y, xh)
    mine = pl.ds(pl.multiple_of(z * 64, 64), 64)

    def piece(o, s):
        return PF.at[order[o], :, pl.ds(pl.multiple_of(s * 64, 64), 64), :]

    def gather_step(o, t):
        if t == 0:
            for h in range(2):
                got(PF.at[order[o], :, mine, pl.ds(BLK * h, BLK)], t_r.at[2 * order[o] + h])
        elif t < 4:
            got(piece(o, at_z(-t)), g_r.at[0, t - 1, o])
            got(piece(o, at_z(t)), g_r.at[1, t - 1, o])
        else:
            got(piece(o, at_z(4)), g_r.at[0 if o < 2 else 1, 3, o])
        if t < 3 or (t == 3 and o < 2):
            src = piece(o, at_z(-t))
            send(src, src, g_s.at[0, t, o], g_r.at[0, t, o], right)
        if t < 3 or (t == 3 and o >= 2):
            src = piece(o, at_z(t))
            send(src, src, g_s.at[1, t, o], g_r.at[1, t, o], left)

    def scale_of(top):
        top = jnp.maximum(jnp.max(top, axis=0, keepdims=True), 1e-30)
        return LIMIT / top, top * (1.0 / LIMIT)

    def first(half):
        return xlo if half == 0 else 1 - xlo

    def region(ref, part, theirs=0, cols=slice(None)):
        pair = pl.ds(2 * first(theirs if part == 0 else 1 - theirs), 2)
        return ref.at[pair, (slice(0, 512), slice(0, 256), slice(256, 512))[part], cols]

    def tiles(part):
        return (4, 2, 2)[part]

    def where_is(part, i):
        if part == 0:
            return 2 * first(0) + i // 2, pl.ds(pl.multiple_of(lax.rem(i, 2) * 256, 256), 256)
        return 2 * first(1) + i, pl.ds(256 * (part - 1), 256)

    def packed(i):
        return pl.ds(pl.multiple_of(i * 256, 256), 256)

    def product(o, part):
        b = PF[order[o]].reshape(2048, 256)

        def tile(i, top):
            k, r = where_is(part, i)
            d = jnp.dot(A4[k, r, :], b, preferred_element_type=F32)
            if o < 3 or part == 2:
                TMP[packed(i), :] = d
                return jnp.maximum(top, jnp.max(jnp.abs(d).reshape(32, 8, 256), axis=0))
            XT[k, r, :] = d
            return top

        top = lax.fori_loop(0, tiles(part), tile, jnp.zeros((8, 256), F32))
        if part == 2:
            inv, back = scale_of(top)
            inv = jnp.where(xh == 0, inv[:, BLK:], inv[:, :BLK])
            back = jnp.where(xh == 0, back[:, BLK:], back[:, :BLK])
            GSQ[o] = jnp.broadcast_to(back, (8, BLK))

            @pl.loop(0, 2)
            def _(i):
                GQ[o, packed(i), :] = jnp.round(TMP[packed(i), give] * inv).astype(jnp.int16)
                XK[o, packed(i), :] = TMP[packed(i), keep]

            to = dev(z, q, y, 1 - xh)
            send(GSQ.at[o], GSR.at[o], b_s.at[1, o], b_r.at[1, o], to)
            send(GQ.at[o], GR.at[o], b_s.at[0, o], b_r.at[0, o], to)
        elif o < 3:
            inv, back = scale_of(top)
            SQ[o, part] = jnp.broadcast_to(back, (8, 256))

            @pl.loop(0, tiles(part))
            def _(i):
                k, r = where_is(part, i)
                XQ[o, k, r, :] = jnp.round(TMP[packed(i), :] * inv).astype(jnp.int16)

            to = dev(z, q, order[o], xh)
            send(SQ.at[o, part], SR.at[o, part], x_s.at[1, o, part], x_r.at[1, o, part], to)
            send(region(XQ.at[o], part), region(XR.at[o], part), x_s.at[0, o, part], x_r.at[0, o, part], to)

    def pair_sum(o):
        got(GSR.at[o], b_r.at[1, o])
        got(GR.at[o], b_r.at[0, o])
        scale = GSR[o, 0:1, :]

        def tile(i, top):
            s = XK[o, packed(i), :] + GR[o, packed(i), :].astype(F32) * scale
            XK[o, packed(i), :] = s
            return jnp.maximum(top, jnp.max(jnp.abs(s).reshape(32, 8, BLK), axis=0))

        top = lax.fori_loop(0, 2, tile, jnp.zeros((8, BLK), F32))
        if o < 3:
            inv, back = scale_of(top)
            YSQ[o] = jnp.broadcast_to(back, (8, BLK))

            @pl.loop(0, 2)
            def _(i):
                YQ[o, packed(i), :] = jnp.round(XK[o, packed(i), :] * inv).astype(jnp.int16)

            to = dev(z, q, order[o], xh)
            send(YSQ.at[o], YSR.at[o], x_s.at[1, o, 2], x_r.at[1, o, 2], to)
            send(YQ.at[o], YR.at[o], x_s.at[0, o, 2], x_r.at[0, o, 2], to)

    keep = pl.ds(pl.multiple_of(xh * BLK, BLK), BLK)
    give = pl.ds(pl.multiple_of((1 - xh) * BLK, BLK), BLK)

    def add_up(part):
        for o in range(3):
            got(SR.at[o, part], x_r.at[1, o, part])
            got(region(XR.at[o], part), x_r.at[0, o, part])

        def tile(i, top):
            k, r = where_is(part, i)
            s = XT[k, r, :]
            for o in range(3):
                s += XR[o, k, r, :].astype(F32) * SR[o, part, 0:1, :]
            XT[k, r, :] = s
            return jnp.maximum(top, jnp.max(jnp.abs(s).reshape(32, 8, 256), axis=0))

        top = lax.fori_loop(0, tiles(part), tile, jnp.zeros((8, 256), F32))
        inv, back = scale_of(top)
        inv = jnp.where(xh == 0, inv[:, BLK:], inv[:, :BLK])
        back = jnp.where(xh == 0, back[:, BLK:], back[:, :BLK])
        HSQ[part] = jnp.broadcast_to(back, (8, BLK))

        @pl.loop(0, tiles(part))
        def _(i):
            k, r = where_is(part, i)
            HQ[k, r, :] = jnp.round(XT[k, r, give] * inv).astype(jnp.int16)

        to = dev(z, q, y, 1 - xh)
        send(HSQ.at[part], HSR.at[part], h_s.at[1, part], h_r.at[1, part], to)
        send(region(HQ, part), region(HR, part), h_s.at[0, part], h_r.at[0, part], to)

    def lanes(who):
        return pl.ds(pl.multiple_of(who * BLK, BLK), BLK)

    def finish_x(part):
        if part < 2:
            got(HSR.at[part], h_r.at[1, part])
            got(region(HR, part), h_r.at[0, part])
        else:
            for o in range(3):
                got(YSR.at[o], x_r.at[1, o, 2])
                got(YR.at[o], x_r.at[0, o, 2])
        slot = lax.broadcasted_iota(jnp.int32, (256, BLK), 0)
        for i in range(tiles(part)):
            k, r = where_is(part, i)
            if part < 2:
                s = XT[k, r, keep] + HR[k, r, :].astype(F32) * HSR[part, 0:1, :]
            else:
                s = XK[3, packed(i), :]
                for o in range(3):
                    s += YR[o, packed(i), :].astype(F32) * YSR[o, 0:1, :]
            start = 256 * (i % 2) if part == 0 else 256 * (part - 1)
            XF[k, r, lanes(q)] = jnp.where(slot + start < cnt[4 * z + k] * BLK, -s, 0.0).astype(BF)
        src = region(XF, part, 0, lanes(q))
        send(src, src, f_s.at[0, part], f_r.at[0, part], dev(z, qx, y, xh))
        send(src, src, f_s.at[1, part], f_r.at[1, part], dev(z, qc, y, xh))

    def pass_x(part):
        src = region(XF, part, 1, lanes(qx))
        got(src, f_r.at[0, part])
        send(src, src, f_s.at[2, part], f_r.at[2, part], dev(z, qc, y, xh))

    def got_core(part):
        got(region(XF, part, 0, lanes(qc)), f_r.at[1, part])

    def got_far(part):
        got(region(XF, part, 1, lanes(qd)), f_r.at[2, part])

    def half_lanes(half):
        return pl.ds(pl.multiple_of(256 * first(half), 256), 256)

    def diagonal(half):
        x = XF[:, :, half_lanes(half)].reshape(2048, 256)
        for t in (1, 2, 0, 3):
            DP[half, t] = jnp.dot(PZT[256 * t:256 * (t + 1), :], x, preferred_element_type=F32)
            if t == 2:
                ring(half, 0)

    def ring(half, step):
        for way in range(2):
            hops = 4 if half == way else 3
            if step > hops:
                continue
            k = hops - step - 1 if way == 0 else 7 - hops + step
            if step == hops:
                k = 7
            v = DP[half, k // 2, BLK * (k % 2):BLK * (k % 2 + 1), :]
            if step > 0:
                got(DSR.at[half, way, step - 1], d_r.at[1, half, way, step - 1])
                got(DR.at[half, way, step - 1], d_r.at[0, half, way, step - 1])
                v += DR[half, way, step - 1].astype(F32) * DSR[half, way, step - 1, 0:1, :]
            if step == hops:
                DP[half, 3, BLK:, :] = v
                continue
            inv, back = scale_of(jnp.abs(v))
            DSQ[half, way, step] = jnp.broadcast_to(back, (8, 256))
            DQ[half, way, step] = jnp.round(v * inv).astype(jnp.int16)
            to = right if way == 0 else left
            send(DSQ.at[half, way, step], DSR.at[half, way, step],
                 d_s.at[1, half, way, step], d_r.at[1, half, way, step], to)
            send(DQ.at[half, way, step], DR.at[half, way, step],
                 d_s.at[0, half, way, step], d_r.at[0, half, way, step], to)

    rows_over(0)
    for r in range(EARLY, 4):
        send_a(r)

    def own_rows():
        own_a.wait()
        for r in range(4):
            got(A4.at[qc, pl.ds(r * BLK, BLK)], a_r.at[0, r])

    def other_rows(part):
        for r in (2 * part - 2, 2 * part - 1):
            got(A4.at[qd, pl.ds(r * BLK, BLK)], a_r.at[2, r])

    gather_step(0, 0)
    gather_step(1, 0)
    gather_step(0, 1)
    gather_step(1, 1)
    rows_over(1)
    gather_step(0, 2)
    gather_step(1, 2)
    gather_step(0, 3)
    gather_step(1, 3)
    gather_step(2, 0)
    gather_step(3, 0)
    forward_a(0)
    gather_step(0, 4)
    own_rows()
    product(0, 0)
    gather_step(2, 1)
    gather_step(3, 1)
    gather_step(1, 4)
    product(1, 0)
    forward_a(1)
    gather_step(2, 2)
    gather_step(3, 2)
    other_rows(1)
    product(0, 1)
    gather_step(2, 3)
    gather_step(3, 3)
    product(1, 1)
    forward_a(2)
    gather_step(2, 4)
    product(2, 0)
    product(2, 1)
    gather_step(3, 4)
    product(3, 0)
    product(3, 1)
    forward_a(3)
    other_rows(2)
    product(0, 2)
    product(1, 2)
    add_up(0)
    product(2, 2)
    pair_sum(0)
    product(3, 2)
    pair_sum(1)
    add_up(1)
    pair_sum(2)
    rows_over(2)
    finish_x(0)
    pass_x(0)
    pair_sum(3)
    finish_x(1)
    pass_x(1)
    finish_x(2)
    rows_over(3)
    got_core(0)
    got_core(1)
    got_core(2)
    diagonal(0)
    pass_x(2)
    got_far(0)
    got_far(1)
    got_far(2)
    diagonal(1)
    ring(0, 1)
    ring(1, 1)
    ring(0, 2)
    ring(1, 2)
    ring(0, 3)
    ring(1, 3)
    ring(0, 4)
    ring(1, 4)
    off[...] = XF[q]
    for half in range(2):
        cols = half_lanes(half)
        dout[:, cols] = diag[:, cols].astype(F32) - DP[half, 3, BLK:, :]

    for cp in sends:
        cp.wait_send()

    @pl.when(z != c)
    def _():
        there.wait_send()


def per_device(panel, anc_inverse, diag_inverse, block_counts):
    vmem = functools.partial(pl.BlockSpec, memory_space=pltpu.VMEM)
    dma = pltpu.SemaphoreType.DMA
    i16 = jnp.int16
    return pl.pallas_call(
        kernel,
        out_shape=(
            jax.ShapeDtypeStruct((512, 512), BF),
            jax.ShapeDtypeStruct((BLK, 512), F32),
        ),
        in_specs=[pl.BlockSpec(memory_space=pltpu.SMEM), vmem(), vmem(), vmem()],
        out_specs=(vmem(), vmem()),
        scratch_shapes=[
            pltpu.VMEM((8, 4, 512, BLK), BF),
            pltpu.VMEM((4, 4, 512, 256), BF),
            pltpu.VMEM((4, 512, 2048), BF),
            pltpu.VMEM((4, 512, 256), F32),
            pltpu.VMEM((1024, 256), F32),
            pltpu.VMEM((2, 4, 256, 256), F32),
            pltpu.VMEM((3, 4, 512, 256), i16),
            pltpu.VMEM((3, 4, 512, 256), i16),
            pltpu.VMEM((3, 2, 8, 256), F32),
            pltpu.VMEM((3, 2, 8, 256), F32),
            pltpu.VMEM((4, 512, BLK), i16),
            pltpu.VMEM((4, 512, BLK), i16),
            pltpu.VMEM((4, 8, BLK), F32),
            pltpu.VMEM((4, 8, BLK), F32),
            pltpu.VMEM((4, 512, BLK), F32),
            pltpu.VMEM((3, 512, BLK), i16),
            pltpu.VMEM((3, 512, BLK), i16),
            pltpu.VMEM((3, 8, BLK), F32),
            pltpu.VMEM((3, 8, BLK), F32),
            pltpu.VMEM((4, 512, BLK), i16),
            pltpu.VMEM((4, 512, BLK), i16),
            pltpu.VMEM((2, 8, BLK), F32),
            pltpu.VMEM((2, 8, BLK), F32),
            pltpu.VMEM((4, 512, 512), BF),
            pltpu.VMEM((1024, 2048), BF),
            pltpu.VMEM((2, 2, 4, BLK, 256), i16),
            pltpu.VMEM((2, 2, 4, BLK, 256), i16),
            pltpu.VMEM((2, 2, 4, 8, 256), F32),
            pltpu.VMEM((2, 2, 4, 8, 256), F32),
            pltpu.VMEM((512, 512), BF),
            dma((3, 4)), dma((3, 4)), dma((3,)), dma((3,)), dma((8,)), dma((8,)),
            dma((2, 4, 4)), dma((2, 4, 4)), dma((7,)), dma((7,)), dma((2, 3, 3)), dma((2, 3, 3)), dma((2, 4)), dma((2, 4)),
            dma((2, 2)), dma((2, 2)), dma((3, 3)), dma((3, 3)), dma((2, 2, 2, 4)), dma((2, 2, 2, 4)), dma((1,)),
        ],
        compiler_params=pltpu.CompilerParams(
            collective_id=0, has_side_effects=True, vmem_limit_bytes=56 << 20
        ),
        cost_estimate=pl.CostEstimate(
            flops=10_737_418_240, bytes_accessed=4 << 20, transcendentals=0
        ),
        name="selected_inversion",
    )(block_counts, panel, anc_inverse, diag_inverse)


def solution(mesh):
    return jax.shard_map(
        per_device,
        mesh=mesh,
        in_specs=(P("prow", "pcol"), P("prow", "pcol"), P("prow", "pcol"), P()),
        out_specs=(P("prow", "pcol"), P("prow", "pcol")),
        check_vma=False,
    )
```

```python
import functools

import jax
import jax.numpy as jnp
from jax import lax
from jax.experimental import pallas as pl
from jax.experimental.pallas import tpu as pltpu
from jax.sharding import PartitionSpec as P

BLK = 128
MESH = pl.DeviceIdType.MESH
BF = jnp.bfloat16
F32 = jnp.float32
LIMIT = 32000.0
EARLY = 0


def kernel(
    cnt, panel, anc, off, dout,
    PZ, PF, A4, XT, TMP, DP, XQ, XR, SQ, SR, HQ, HR, HSQ, HSR, XF, PZT, DQ, DR, DSQ, DSR, pm,
    a_s, a_r, q_s, q_r, t_s, t_r, g_s, g_r, w_s, w_r, x_s, x_r, h_s, h_r, f_s, f_r, d_s, d_r, loc,
):
    p = lax.axis_index("prow")
    c = lax.axis_index("pcol")
    z, q = p // 4, lax.rem(p, 4)
    xlo, core = q // 2, lax.rem(q, 2)
    y, xh = c // 2, lax.rem(c, 2)
    qc = 2 * xlo + (1 - core)
    qx = 2 * (1 - xlo) + core
    qd = 2 * (1 - xlo) + (1 - core)

    def at_z(k):
        return lax.rem(z + k + 8, 8)

    def at_y(k):
        return lax.rem(y + k + 4, 4)

    def dev(zz, qq, yy, hh):
        return (4 * zz + qq, 2 * yy + hh)

    sends = []

    def send(src, dst, ss, rs, to):
        cp = pltpu.make_async_remote_copy(
            src_ref=src, dst_ref=dst, send_sem=ss, recv_sem=rs, device_id=to, device_id_type=MESH
        )
        cp.start()
        sends.append(cp)

    def got(dst, rs):
        pltpu.make_async_copy(dst, dst, rs).wait()

    barrier = pltpu.get_barrier_semaphore()
    greet = [(4 * c + q, lax.rem(c + k, 8)) for k in range(1, 8)]
    greet += [dev(at_z(k), q, y, xh) for k in (1, 7)]
    greet += [dev(z, q, at_y(k), xh) for k in (2, 1, 3)]
    greet += [dev(z, q, y, 1 - xh)]
    greet += [dev(z, k, y, xh) for k in (qd, qx, qc)]
    for who in greet:
        pl.semaphore_signal(barrier, inc=1, device_id=who, device_id_type=MESH)

    @pl.when(z != c)
    def _():
        pl.semaphore_signal(barrier, inc=1, device_id=(4 * c + q, c), device_id_type=MESH)

    count = cnt[p]
    rows = lax.broadcasted_iota(jnp.int32, (512, 512), 0)
    pm[...] = jnp.where(rows < count * BLK, panel[...].astype(F32), 0.0).astype(BF)
    PZ[c, q] = pm[:, pl.ds(pl.multiple_of(q * BLK, BLK), BLK)]

    pl.semaphore_wait(barrier, jnp.where(z == c, 16, 17))

    for i, k in enumerate((qx, qd, qc)):
        send(
            pm.at[:, pl.ds(pl.multiple_of(k * BLK, BLK), BLK)], PZ.at[c, q],
            q_s.at[i], q_r.at[i], dev(z, k, y, xh),
        )
    own_a = pltpu.make_async_copy(anc, A4.at[q], loc.at[0])
    own_a.start()

    def send_a(r):
        part = pl.ds(r * BLK, BLK)
        send(anc.at[part], A4.at[q, part], a_s.at[1, r], a_r.at[1, r], dev(z, qx, y, xh))
        send(anc.at[part], A4.at[q, part], a_s.at[0, r], a_r.at[0, r], dev(z, qc, y, xh))

    def forward_a(r):
        part = pl.ds(r * BLK, BLK)
        got(A4.at[qx, part], a_r.at[1, r])
        send(A4.at[qx, part], A4.at[qx, part], a_s.at[2, r], a_r.at[2, r], dev(z, qc, y, xh))

    for r in range(EARLY):
        send_a(r)
    for i, k in enumerate((qx, qd, qc)):
        got(PZ.at[c, k], q_r.at[i])

    for k in range(8):
        s = at_z(k + 1)
        part = pl.ds(pl.multiple_of(s * 64, 64), 64)
        src = PZ.at[c, :, part]
        dst = PF.at[y, :, part, pl.ds(pl.multiple_of(xh * BLK, BLK), BLK)]
        if k < 7:
            send(src, dst, t_s.at[k], t_r.at[c], dev(s, q, z // 2, lax.rem(z, 2)))
        else:
            there = pltpu.make_async_remote_copy(
                src_ref=src, dst_ref=dst, send_sem=t_s.at[k], recv_sem=t_r.at[c],
                device_id=dev(s, q, z // 2, lax.rem(z, 2)), device_id_type=MESH,
            )
            here = pltpu.make_async_copy(src, dst, t_r.at[c])

            @pl.when(z != c)
            def _():
                there.start()

            @pl.when(z == c)
            def _():
                here.start()

    def rows_over(stage):
        up_to, down_to = dev(z, q, at_y(1), xh), dev(z, q, at_y(3), xh)
        if stage == 0:
            send(PZ.at[c], PZ.at[c], w_s.at[1], w_r.at[1], up_to)
            send(PZ.at[c], PZ.at[c], w_s.at[2], w_r.at[2], down_to)
            send(PZ.at[c], PZ.at[c], w_s.at[0], w_r.at[0], dev(z, q, y, 1 - xh))
        if stage == 1:
            other = 2 * y + 1 - xh
            got(PZ.at[other], w_r.at[0])
            send(PZ.at[other], PZ.at[other], w_s.at[3], w_r.at[3], up_to)
            send(PZ.at[other], PZ.at[other], w_s.at[4], w_r.at[4], down_to)
        if stage == 2:
            down, up = at_y(-1), at_y(1)
            got(PZ.at[2 * down + xh], w_r.at[1])
            got(PZ.at[2 * up + xh], w_r.at[2])
            got(PZ.at[2 * down + 1 - xh], w_r.at[3])
            got(PZ.at[2 * up + 1 - xh], w_r.at[4])
            fd, fu = PZ.at[2 * down], PZ.at[2 * up + 1]
            send(fd, fd, w_s.at[5], w_r.at[5], up_to)
            send(fu, fu, w_s.at[6], w_r.at[6], down_to)
        if stage == 3:
            far = at_y(2)
            got(PZ.at[2 * far], w_r.at[5])
            got(PZ.at[2 * far + 1], w_r.at[6])
            for k in range(8):
                PZT[BLK * k:BLK * (k + 1), :] = PZ[at_z(k + 1)].reshape(2048, BLK).T

    order = [at_y(2), at_y(1), at_y(3), y]
    right, left = dev(at_z(1), q, y, xh), dev(at_z(7), q, y, xh)
    mine = pl.ds(pl.multiple_of(z * 64, 64), 64)

    def piece(o, s):
        return PF.at[order[o], :, pl.ds(pl.multiple_of(s * 64, 64), 64), :]

    def gather_step(o, t):
        if t == 0:
            for h in range(2):
                got(PF.at[order[o], :, mine, pl.ds(BLK * h, BLK)], t_r.at[2 * order[o] + h])
        elif t < 4:
            got(piece(o, at_z(-t)), g_r.at[0, t - 1, o])
            got(piece(o, at_z(t)), g_r.at[1, t - 1, o])
        else:
            got(piece(o, at_z(4)), g_r.at[0 if o < 2 else 1, 3, o])
        if t < 3 or (t == 3 and o < 2):
            src = piece(o, at_z(-t))
            send(src, src, g_s.at[0, t, o], g_r.at[0, t, o], right)
        if t < 3 or (t == 3 and o >= 2):
            src = piece(o, at_z(t))
            send(src, src, g_s.at[1, t, o], g_r.at[1, t, o], left)

    def scale_of(top):
        top = jnp.maximum(jnp.max(top, axis=0, keepdims=True), 1e-30)
        return LIMIT / top, top * (1.0 / LIMIT)

    def first(half):
        return xlo if half == 0 else 1 - xlo

    def region(ref, part, theirs=0, cols=slice(None)):
        pair = pl.ds(2 * first(theirs if part == 0 else 1 - theirs), 2)
        return ref.at[pair, (slice(0, 512), slice(0, 256), slice(256, 512))[part], cols]

    def tiles(part):
        return (4, 2, 2)[part]

    def where_is(part, i):
        if part == 0:
            return 2 * first(0) + i // 2, pl.ds(pl.multiple_of(lax.rem(i, 2) * 256, 256), 256)
        return 2 * first(1) + i, pl.ds(256 * (part - 1), 256)

    def packed(i):
        return pl.ds(pl.multiple_of(i * 256, 256), 256)

    def product(o, part):
        b = PF[order[o]].reshape(2048, 256)

        def tile(i, top):
            k, r = where_is(part, i)
            d = jnp.dot(A4[k, r, :], b, preferred_element_type=F32)
            if o < 3:
                TMP[packed(i), :] = d
                return jnp.maximum(top, jnp.max(jnp.abs(d).reshape(32, 8, 256), axis=0))
            XT[k, r, :] = d
            return top

        top = lax.fori_loop(0, tiles(part), tile, jnp.zeros((8, 256), F32))
        if o < 3:
            inv, back = scale_of(top)
            SQ[o, part] = jnp.broadcast_to(back, (8, 256))

            @pl.loop(0, tiles(part))
            def _(i):
                k, r = where_is(part, i)
                XQ[o, k, r, :] = jnp.round(TMP[packed(i), :] * inv).astype(jnp.int16)

            to = dev(z, q, order[o], xh)
            send(SQ.at[o, part], SR.at[o, part], x_s.at[1, o, part], x_r.at[1, o, part], to)
            send(region(XQ.at[o], part), region(XR.at[o], part), x_s.at[0, o, part], x_r.at[0, o, part], to)

    keep = pl.ds(pl.multiple_of(xh * BLK, BLK), BLK)
    give = pl.ds(pl.multiple_of((1 - xh) * BLK, BLK), BLK)

    def add_up(part):
        for o in range(3):
            got(SR.at[o, part], x_r.at[1, o, part])
            got(region(XR.at[o], part), x_r.at[0, o, part])

        def tile(i, top):
            k, r = where_is(part, i)
            s = XT[k, r, :]
            for o in range(3):
                s += XR[o, k, r, :].astype(F32) * SR[o, part, 0:1, :]
            XT[k, r, :] = s
            return jnp.maximum(top, jnp.max(jnp.abs(s).reshape(32, 8, 256), axis=0))

        top = lax.fori_loop(0, tiles(part), tile, jnp.zeros((8, 256), F32))
        inv, back = scale_of(top)
        inv = jnp.where(xh == 0, inv[:, BLK:], inv[:, :BLK])
        back = jnp.where(xh == 0, back[:, BLK:], back[:, :BLK])
        HSQ[part] = jnp.broadcast_to(back, (8, BLK))

        @pl.loop(0, tiles(part))
        def _(i):
            k, r = where_is(part, i)
            HQ[k, r, :] = jnp.round(XT[k, r, give] * inv).astype(jnp.int16)

        to = dev(z, q, y, 1 - xh)
        send(HSQ.at[part], HSR.at[part], h_s.at[1, part], h_r.at[1, part], to)
        send(region(HQ, part), region(HR, part), h_s.at[0, part], h_r.at[0, part], to)

    def lanes(who):
        return pl.ds(pl.multiple_of(who * BLK, BLK), BLK)

    def finish_x(part):
        got(HSR.at[part], h_r.at[1, part])
        got(region(HR, part), h_r.at[0, part])
        slot = lax.broadcasted_iota(jnp.int32, (256, BLK), 0)
        for i in range(tiles(part)):
            k, r = where_is(part, i)
            s = XT[k, r, keep] + HR[k, r, :].astype(F32) * HSR[part, 0:1, :]
            start = 256 * (i % 2) if part == 0 else 256 * (part - 1)
            XF[k, r, lanes(q)] = jnp.where(slot + start < cnt[4 * z + k] * BLK, -s, 0.0).astype(BF)
        src = region(XF, part, 0, lanes(q))
        send(src, src, f_s.at[0, part], f_r.at[0, part], dev(z, qx, y, xh))
        send(src, src, f_s.at[1, part], f_r.at[1, part], dev(z, qc, y, xh))

    def pass_x(part):
        src = region(XF, part, 1, lanes(qx))
        got(src, f_r.at[0, part])
        send(src, src, f_s.at[2, part], f_r.at[2, part], dev(z, qc, y, xh))

    def got_core(part):
        got(region(XF, part, 0, lanes(qc)), f_r.at[1, part])

    def got_far(part):
        got(region(XF, part, 1, lanes(qd)), f_r.at[2, part])

    def half_lanes(half):
        return pl.ds(pl.multiple_of(256 * first(half), 256), 256)

    def diagonal(half):
        x = XF[:, :, half_lanes(half)].reshape(2048, 256)
        for t in (1, 2, 0, 3):
            DP[half, t] = jnp.dot(PZT[256 * t:256 * (t + 1), :], x, preferred_element_type=F32)
            if t == 2:
                ring(half, 0)

    def ring(half, step):
        for way in range(2):
            hops = 4 if half == way else 3
            if step > hops:
                continue
            k = hops - step - 1 if way == 0 else 7 - hops + step
            if step == hops:
                k = 7
            v = DP[half, k // 2, BLK * (k % 2):BLK * (k % 2 + 1), :]
            if step > 0:
                got(DSR.at[half, way, step - 1], d_r.at[1, half, way, step - 1])
                got(DR.at[half, way, step - 1], d_r.at[0, half, way, step - 1])
                v += DR[half, way, step - 1].astype(F32) * DSR[half, way, step - 1, 0:1, :]
            if step == hops:
                DP[half, 3, BLK:, :] = v
                continue
            inv, back = scale_of(jnp.abs(v))
            DSQ[half, way, step] = jnp.broadcast_to(back, (8, 256))
            DQ[half, way, step] = jnp.round(v * inv).astype(jnp.int16)
            to = right if way == 0 else left
            send(DSQ.at[half, way, step], DSR.at[half, way, step],
                 d_s.at[1, half, way, step], d_r.at[1, half, way, step], to)
            send(DQ.at[half, way, step], DR.at[half, way, step],
                 d_s.at[0, half, way, step], d_r.at[0, half, way, step], to)

    rows_over(0)
    for r in range(EARLY, 4):
        send_a(r)

    def own_rows():
        own_a.wait()
        for r in range(4):
            got(A4.at[qc, pl.ds(r * BLK, BLK)], a_r.at[0, r])

    def other_rows(part):
        for r in (2 * part - 2, 2 * part - 1):
            got(A4.at[qd, pl.ds(r * BLK, BLK)], a_r.at[2, r])

    gather_step(0, 0)
    gather_step(1, 0)
    gather_step(0, 1)
    gather_step(1, 1)
    rows_over(1)
    gather_step(0, 2)
    gather_step(1, 2)
    gather_step(0, 3)
    gather_step(1, 3)
    gather_step(2, 0)
    gather_step(3, 0)
    forward_a(0)
    gather_step(0, 4)
    own_rows()
    product(0, 0)
    gather_step(2, 1)
    gather_step(3, 1)
    gather_step(1, 4)
    product(1, 0)
    forward_a(1)
    gather_step(2, 2)
    gather_step(3, 2)
    other_rows(1)
    product(0, 1)
    gather_step(2, 3)
    gather_step(3, 3)
    product(1, 1)
    forward_a(2)
    gather_step(2, 4)
    product(2, 0)
    product(2, 1)
    gather_step(3, 4)
    product(3, 0)
    product(3, 1)
    forward_a(3)
    other_rows(2)
    product(0, 2)
    product(1, 2)
    product(2, 2)
    rows_over(2)
    add_up(0)
    product(3, 2)
    add_up(1)
    finish_x(0)
    add_up(2)
    pass_x(0)
    finish_x(1)
    pass_x(1)
    finish_x(2)
    rows_over(3)
    got_core(0)
    got_core(1)
    got_core(2)
    diagonal(0)
    pass_x(2)
    got_far(0)
    got_far(1)
    got_far(2)
    diagonal(1)
    ring(0, 1)
    ring(1, 1)
    ring(0, 2)
    ring(1, 2)
    ring(0, 3)
    ring(1, 3)
    ring(0, 4)
    ring(1, 4)
    off[...] = XF[q]
    for half in range(2):
        cols = half_lanes(half)
        dout[:, cols] = DP[half, 3, BLK:, :]

    for cp in sends:
        cp.wait_send()

    @pl.when(z != c)
    def _():
        there.wait_send()


def finish(off, total, diag, off_out, diag_out):
    off_out[...] = off[...]
    diag_out[...] = diag[...].astype(F32) - total[...]


def per_device(panel, anc_inverse, diag_inverse, block_counts):
    vmem = functools.partial(pl.BlockSpec, memory_space=pltpu.VMEM)
    dma = pltpu.SemaphoreType.DMA
    i16 = jnp.int16
    off, total = pl.pallas_call(
        kernel,
        out_shape=(
            jax.ShapeDtypeStruct((512, 512), BF),
            jax.ShapeDtypeStruct((BLK, 512), F32),
        ),
        in_specs=[pl.BlockSpec(memory_space=pltpu.SMEM), vmem(), vmem()],
        out_specs=(vmem(), vmem()),
        scratch_shapes=[
            pltpu.VMEM((8, 4, 512, BLK), BF),
            pltpu.VMEM((4, 4, 512, 256), BF),
            pltpu.VMEM((4, 512, 2048), BF),
            pltpu.VMEM((4, 512, 256), F32),
            pltpu.VMEM((1024, 256), F32),
            pltpu.VMEM((2, 4, 256, 256), F32),
            pltpu.VMEM((3, 4, 512, 256), i16),
            pltpu.VMEM((3, 4, 512, 256), i16),
            pltpu.VMEM((3, 3, 8, 256), F32),
            pltpu.VMEM((3, 3, 8, 256), F32),
            pltpu.VMEM((4, 512, BLK), i16),
            pltpu.VMEM((4, 512, BLK), i16),
            pltpu.VMEM((3, 8, BLK), F32),
            pltpu.VMEM((3, 8, BLK), F32),
            pltpu.VMEM((4, 512, 512), BF),
            pltpu.VMEM((1024, 2048), BF),
            pltpu.VMEM((2, 2, 4, BLK, 256), i16),
            pltpu.VMEM((2, 2, 4, BLK, 256), i16),
            pltpu.VMEM((2, 2, 4, 8, 256), F32),
            pltpu.VMEM((2, 2, 4, 8, 256), F32),
            pltpu.VMEM((512, 512), BF),
            dma((3, 4)), dma((3, 4)), dma((3,)), dma((3,)), dma((8,)), dma((8,)),
            dma((2, 4, 4)), dma((2, 4, 4)), dma((7,)), dma((7,)), dma((2, 3, 3)), dma((2, 3, 3)),
            dma((2, 3)), dma((2, 3)), dma((3, 3)), dma((3, 3)), dma((2, 2, 2, 4)), dma((2, 2, 2, 4)), dma((1,)),
        ],
        compiler_params=pltpu.CompilerParams(
            collective_id=0, has_side_effects=True, vmem_limit_bytes=56 << 20
        ),
        cost_estimate=pl.CostEstimate(
            flops=10_737_418_240, bytes_accessed=4 << 20, transcendentals=0
        ),
        name="selected_inversion",
    )(block_counts, panel, anc_inverse)
    return pl.pallas_call(
        finish,
        out_shape=(
            jax.ShapeDtypeStruct((512, 512), BF),
            jax.ShapeDtypeStruct((BLK, 512), F32),
        ),
        in_specs=[vmem()] * 3,
        out_specs=(vmem(), vmem()),
        name="diagonal_update",
    )(off, total, diag_inverse)


def solution(mesh):
    return jax.shard_map(
        per_device,
        mesh=mesh,
        in_specs=(P("prow", "pcol"), P("prow", "pcol"), P("prow", "pcol"), P()),
        out_specs=(P("prow", "pcol"), P("prow", "pcol")),
        check_vma=False,
    )
```

```python
import functools

import jax
import jax.numpy as jnp
from jax import lax
from jax.experimental import pallas as pl
from jax.experimental.pallas import tpu as pltpu
from jax.sharding import PartitionSpec as P

BLK = 128
MESH = pl.DeviceIdType.MESH
BF = jnp.bfloat16
F32 = jnp.float32
LIMIT = 32000.0
EARLY = 0


def kernel(
    cnt, panel, anc, off, dout,
    PZ, PF, A4, XT, TMP, DP, XQ, XR, SQ, SR, HQ, HR, HSQ, HSR, XF, PZT, DQ, DR, DSQ, DSR, pm,
    a_s, a_r, q_s, q_r, t_s, t_r, g_s, g_r, w_s, w_r, x_s, x_r, h_s, h_r, f_s, f_r, d_s, d_r, loc,
):
    p = lax.axis_index("prow")
    c = lax.axis_index("pcol")
    z, q = p // 4, lax.rem(p, 4)
    xlo, core = q // 2, lax.rem(q, 2)
    y, xh = c // 2, lax.rem(c, 2)
    qc = 2 * xlo + (1 - core)
    qx = 2 * (1 - xlo) + core
    qd = 2 * (1 - xlo) + (1 - core)

    def at_z(k):
        return lax.rem(z + k + 8, 8)

    def at_y(k):
        return lax.rem(y + k + 4, 4)

    def dev(zz, qq, yy, hh):
        return (4 * zz + qq, 2 * yy + hh)

    sends = []

    def send(src, dst, ss, rs, to):
        cp = pltpu.make_async_remote_copy(
            src_ref=src, dst_ref=dst, send_sem=ss, recv_sem=rs, device_id=to, device_id_type=MESH
        )
        cp.start()
        sends.append(cp)

    def got(dst, rs):
        pltpu.make_async_copy(dst, dst, rs).wait()

    barrier = pltpu.get_barrier_semaphore()
    greet = [(4 * c + q, lax.rem(c + k, 8)) for k in range(1, 8)]
    greet += [dev(at_z(k), q, y, xh) for k in (1, 7)]
    greet += [dev(z, q, at_y(k), xh) for k in (2, 1, 3)]
    greet += [dev(z, q, y, 1 - xh)]
    greet += [dev(z, k, y, xh) for k in (qd, qx, qc)]
    for who in greet:
        pl.semaphore_signal(barrier, inc=1, device_id=who, device_id_type=MESH)

    @pl.when(z != c)
    def _():
        pl.semaphore_signal(barrier, inc=1, device_id=(4 * c + q, c), device_id_type=MESH)

    count = cnt[p]
    rows = lax.broadcasted_iota(jnp.int32, (512, 512), 0)
    pm[...] = jnp.where(rows < count * BLK, panel[...].astype(F32), 0.0).astype(BF)
    PZ[c, q] = pm[:, pl.ds(pl.multiple_of(q * BLK, BLK), BLK)]

    pl.semaphore_wait(barrier, jnp.where(z == c, 16, 17))

    for i, k in enumerate((qx, qd, qc)):
        send(
            pm.at[:, pl.ds(pl.multiple_of(k * BLK, BLK), BLK)], PZ.at[c, q],
            q_s.at[i], q_r.at[i], dev(z, k, y, xh),
        )
    own_a = pltpu.make_async_copy(anc, A4.at[q], loc.at[0])
    own_a.start()

    def send_a(r):
        part = pl.ds(r * BLK, BLK)
        send(anc.at[part], A4.at[q, part], a_s.at[1, r], a_r.at[1, r], dev(z, qx, y, xh))
        send(anc.at[part], A4.at[q, part], a_s.at[0, r], a_r.at[0, r], dev(z, qc, y, xh))

    def forward_a(r):
        part = pl.ds(r * BLK, BLK)
        got(A4.at[qx, part], a_r.at[1, r])
        send(A4.at[qx, part], A4.at[qx, part], a_s.at[2, r], a_r.at[2, r], dev(z, qc, y, xh))

    for r in range(EARLY):
        send_a(r)
    for i, k in enumerate((qx, qd, qc)):
        got(PZ.at[c, k], q_r.at[i])

    for k in range(8):
        s = at_z(k + 1)
        part = pl.ds(pl.multiple_of(s * 64, 64), 64)
        src = PZ.at[c, :, part]
        dst = PF.at[y, :, part, pl.ds(pl.multiple_of(xh * BLK, BLK), BLK)]
        if k < 7:
            send(src, dst, t_s.at[k], t_r.at[c], dev(s, q, z // 2, lax.rem(z, 2)))
        else:
            there = pltpu.make_async_remote_copy(
                src_ref=src, dst_ref=dst, send_sem=t_s.at[k], recv_sem=t_r.at[c],
                device_id=dev(s, q, z // 2, lax.rem(z, 2)), device_id_type=MESH,
            )
            here = pltpu.make_async_copy(src, dst, t_r.at[c])

            @pl.when(z != c)
            def _():
                there.start()

            @pl.when(z == c)
            def _():
                here.start()

    def rows_over(stage):
        up_to, down_to = dev(z, q, at_y(1), xh), dev(z, q, at_y(3), xh)
        if stage == 0:
            send(PZ.at[c], PZ.at[c], w_s.at[1], w_r.at[1], up_to)
            send(PZ.at[c], PZ.at[c], w_s.at[2], w_r.at[2], down_to)
        if stage == 1:
            other = 2 * y + 1 - xh
            got(PZ.at[other], w_r.at[0])
            send(PZ.at[other], PZ.at[other], w_s.at[3], w_r.at[3], up_to)
            send(PZ.at[other], PZ.at[other], w_s.at[4], w_r.at[4], down_to)
        if stage == 2:
            down, up = at_y(-1), at_y(1)
            got(PZ.at[2 * down + xh], w_r.at[1])
            got(PZ.at[2 * up + xh], w_r.at[2])
            got(PZ.at[2 * down + 1 - xh], w_r.at[3])
            got(PZ.at[2 * up + 1 - xh], w_r.at[4])
            fd, fu = PZ.at[2 * down], PZ.at[2 * up + 1]
            send(fd, fd, w_s.at[5], w_r.at[5], up_to)
            send(fu, fu, w_s.at[6], w_r.at[6], down_to)
        if stage == 3:
            far = at_y(2)
            got(PZ.at[2 * far], w_r.at[5])
            got(PZ.at[2 * far + 1], w_r.at[6])
            for k in range(8):
                PZT[BLK * k:BLK * (k + 1), :] = PZ[at_z(k + 1)].reshape(2048, BLK).T

    order = [at_y(2), at_y(1), at_y(3), y]
    right, left = dev(at_z(1), q, y, xh), dev(at_z(7), q, y, xh)
    mine = pl.ds(pl.multiple_of(z * 64, 64), 64)

    def piece(o, s):
        return PF.at[order[o], :, pl.ds(pl.multiple_of(s * 64, 64), 64), :]

    def gather_step(o, t):
        if t == 0:
            for h in range(2):
                got(PF.at[order[o], :, mine, pl.ds(BLK * h, BLK)], t_r.at[2 * order[o] + h])
        elif t < 4:
            got(piece(o, at_z(-t)), g_r.at[0, t - 1, o])
            got(piece(o, at_z(t)), g_r.at[1, t - 1, o])
        else:
            got(piece(o, at_z(4)), g_r.at[0 if o < 2 else 1, 3, o])
        if t < 3 or (t == 3 and o < 2):
            src = piece(o, at_z(-t))
            send(src, src, g_s.at[0, t, o], g_r.at[0, t, o], right)
        if t < 3 or (t == 3 and o >= 2):
            src = piece(o, at_z(t))
            send(src, src, g_s.at[1, t, o], g_r.at[1, t, o], left)

    def scale_of(top):
        top = jnp.maximum(jnp.max(top, axis=0, keepdims=True), 1e-30)
        return LIMIT / top, top * (1.0 / LIMIT)

    def first(half):
        return xlo if half == 0 else 1 - xlo

    def region(ref, part, theirs=0, cols=slice(None)):
        pair = pl.ds(2 * first(theirs if part == 0 else 1 - theirs), 2)
        return ref.at[pair, (slice(0, 512), slice(0, 256), slice(256, 512))[part], cols]

    def tiles(part):
        return (4, 2, 2)[part]

    def where_is(part, i):
        if part == 0:
            return 2 * first(0) + i // 2, pl.ds(pl.multiple_of(lax.rem(i, 2) * 256, 256), 256)
        return 2 * first(1) + i, pl.ds(256 * (part - 1), 256)

    def packed(i):
        return pl.ds(pl.multiple_of(i * 256, 256), 256)

    def product(o, part):
        b = PF[order[o]].reshape(2048, 256)

        def tile(i, top):
            k, r = where_is(part, i)
            d = jnp.dot(A4[k, r, :], b, preferred_element_type=F32)
            if o < 3:
                TMP[packed(i), :] = d
                return jnp.maximum(top, jnp.max(jnp.abs(d).reshape(32, 8, 256), axis=0))
            XT[k, r, :] = d
            return top

        top = lax.fori_loop(0, tiles(part), tile, jnp.zeros((8, 256), F32))
        if o < 3:
            inv, back = scale_of(top)
            SQ[o, part] = jnp.broadcast_to(back, (8, 256))

            @pl.loop(0, tiles(part))
            def _(i):
                k, r = where_is(part, i)
                XQ[o, k, r, :] = jnp.round(TMP[packed(i), :] * inv).astype(jnp.int16)

            to = dev(z, q, order[o], xh)
            send(SQ.at[o, part], SR.at[o, part], x_s.at[1, o, part], x_r.at[1, o, part], to)
            send(region(XQ.at[o], part), region(XR.at[o], part), x_s.at[0, o, part], x_r.at[0, o, part], to)

    keep = pl.ds(pl.multiple_of(xh * BLK, BLK), BLK)
    give = pl.ds(pl.multiple_of((1 - xh) * BLK, BLK), BLK)

    def add_up(part):
        for o in range(3):
            got(SR.at[o, part], x_r.at[1, o, part])
            got(region(XR.at[o], part), x_r.at[0, o, part])

        def tile(i, top):
            k, r = where_is(part, i)
            s = XT[k, r, :]
            for o in range(3):
                s += XR[o, k, r, :].astype(F32) * SR[o, part, 0:1, :]
            XT[k, r, :] = s
            return jnp.maximum(top, jnp.max(jnp.abs(s).reshape(32, 8, 256), axis=0))

        top = lax.fori_loop(0, tiles(part), tile, jnp.zeros((8, 256), F32))
        inv, back = scale_of(top)
        inv = jnp.where(xh == 0, inv[:, BLK:], inv[:, :BLK])
        back = jnp.where(xh == 0, back[:, BLK:], back[:, :BLK])
        HSQ[part] = jnp.broadcast_to(back, (8, BLK))

        @pl.loop(0, tiles(part))
        def _(i):
            k, r = where_is(part, i)
            HQ[k, r, :] = jnp.round(XT[k, r, give] * inv).astype(jnp.int16)

        to = dev(z, q, y, 1 - xh)
        send(HSQ.at[part], HSR.at[part], h_s.at[1, part], h_r.at[1, part], to)
        send(region(HQ, part), region(HR, part), h_s.at[0, part], h_r.at[0, part], to)

    def lanes(who):
        return pl.ds(pl.multiple_of(who * BLK, BLK), BLK)

    def finish_x(part):
        got(HSR.at[part], h_r.at[1, part])
        got(region(HR, part), h_r.at[0, part])
        slot = lax.broadcasted_iota(jnp.int32, (256, BLK), 0)
        for i in range(tiles(part)):
            k, r = where_is(part, i)
            s = XT[k, r, keep] + HR[k, r, :].astype(F32) * HSR[part, 0:1, :]
            start = 256 * (i % 2) if part == 0 else 256 * (part - 1)
            XF[k, r, lanes(q)] = jnp.where(slot + start < cnt[4 * z + k] * BLK, -s, 0.0).astype(BF)
        src = region(XF, part, 0, lanes(q))
        send(src, src, f_s.at[0, part], f_r.at[0, part], dev(z, qx, y, xh))
        send(src, src, f_s.at[1, part], f_r.at[1, part], dev(z, qc, y, xh))

    def pass_x(part):
        src = region(XF, part, 1, lanes(qx))
        got(src, f_r.at[0, part])
        send(src, src, f_s.at[2, part], f_r.at[2, part], dev(z, qc, y, xh))

    def got_core(part):
        got(region(XF, part, 0, lanes(qc)), f_r.at[1, part])

    def got_far(part):
        got(region(XF, part, 1, lanes(qd)), f_r.at[2, part])

    def half_lanes(half):
        return pl.ds(pl.multiple_of(256 * first(half), 256), 256)

    def diagonal(half):
        x = XF[:, :, half_lanes(half)].reshape(2048, 256)
        for t in (1, 2, 0, 3):
            DP[half, t] = jnp.dot(PZT[256 * t:256 * (t + 1), :], x, preferred_element_type=F32)
            if t == 2:
                ring(half, 0)

    def ring(half, step):
        for way in range(2):
            hops = 4 if half == way else 3
            if step > hops:
                continue
            k = hops - step - 1 if way == 0 else 7 - hops + step
            if step == hops:
                k = 7
            v = DP[half, k // 2, BLK * (k % 2):BLK * (k % 2 + 1), :]
            if step > 0:
                got(DSR.at[half, way, step - 1], d_r.at[1, half, way, step - 1])
                got(DR.at[half, way, step - 1], d_r.at[0, half, way, step - 1])
                v += DR[half, way, step - 1].astype(F32) * DSR[half, way, step - 1, 0:1, :]
            if step == hops:
                DP[half, 3, BLK:, :] = v
                continue
            inv, back = scale_of(jnp.abs(v))
            DSQ[half, way, step] = jnp.broadcast_to(back, (8, 256))
            DQ[half, way, step] = jnp.round(v * inv).astype(jnp.int16)
            to = right if way == 0 else left
            send(DSQ.at[half, way, step], DSR.at[half, way, step],
                 d_s.at[1, half, way, step], d_r.at[1, half, way, step], to)
            send(DQ.at[half, way, step], DR.at[half, way, step],
                 d_s.at[0, half, way, step], d_r.at[0, half, way, step], to)

    rows_over(0)
    for r in range(EARLY, 4):
        send_a(r)
    send(PZ.at[c], PZ.at[c], w_s.at[0], w_r.at[0], dev(z, q, y, 1 - xh))

    def own_rows():
        own_a.wait()
        for r in range(4):
            got(A4.at[qc, pl.ds(r * BLK, BLK)], a_r.at[0, r])

    def other_rows(part):
        for r in (2 * part - 2, 2 * part - 1):
            got(A4.at[qd, pl.ds(r * BLK, BLK)], a_r.at[2, r])

    gather_step(0, 0)
    gather_step(1, 0)
    gather_step(0, 1)
    gather_step(1, 1)
    gather_step(0, 2)
    gather_step(1, 2)
    gather_step(0, 3)
    gather_step(1, 3)
    gather_step(2, 0)
    gather_step(3, 0)
    forward_a(0)
    gather_step(0, 4)
    own_rows()
    product(0, 0)
    gather_step(2, 1)
    gather_step(3, 1)
    gather_step(1, 4)
    product(1, 0)
    forward_a(1)
    gather_step(2, 2)
    gather_step(3, 2)
    other_rows(1)
    product(0, 1)
    gather_step(2, 3)
    gather_step(3, 3)
    product(1, 1)
    forward_a(2)
    gather_step(2, 4)
    product(2, 0)
    product(2, 1)
    gather_step(3, 4)
    product(3, 0)
    product(3, 1)
    forward_a(3)
    other_rows(2)
    product(0, 2)
    product(1, 2)
    product(2, 2)
    rows_over(1)
    add_up(0)
    product(3, 2)
    add_up(1)
    finish_x(0)
    add_up(2)
    rows_over(2)
    pass_x(0)
    finish_x(1)
    pass_x(1)
    finish_x(2)
    rows_over(3)
    got_core(0)
    got_core(1)
    got_core(2)
    diagonal(0)
    pass_x(2)
    got_far(0)
    got_far(1)
    got_far(2)
    diagonal(1)
    ring(0, 1)
    ring(1, 1)
    ring(0, 2)
    ring(1, 2)
    ring(0, 3)
    ring(1, 3)
    ring(0, 4)
    ring(1, 4)
    off[...] = XF[q]
    for half in range(2):
        cols = half_lanes(half)
        dout[:, cols] = DP[half, 3, BLK:, :]

    for cp in sends:
        cp.wait_send()

    @pl.when(z != c)
    def _():
        there.wait_send()


def finish(off, total, diag, off_out, diag_out):
    off_out[...] = off[...]
    diag_out[...] = diag[...].astype(F32) - total[...]


def per_device(panel, anc_inverse, diag_inverse, block_counts):
    vmem = functools.partial(pl.BlockSpec, memory_space=pltpu.VMEM)
    dma = pltpu.SemaphoreType.DMA
    i16 = jnp.int16
    off, total = pl.pallas_call(
        kernel,
        out_shape=(
            jax.ShapeDtypeStruct((512, 512), BF),
            jax.ShapeDtypeStruct((BLK, 512), F32),
        ),
        in_specs=[pl.BlockSpec(memory_space=pltpu.SMEM), vmem(), vmem()],
        out_specs=(vmem(), vmem()),
        scratch_shapes=[
            pltpu.VMEM((8, 4, 512, BLK), BF),
            pltpu.VMEM((4, 4, 512, 256), BF),
            pltpu.VMEM((4, 512, 2048), BF),
            pltpu.VMEM((4, 512, 256), F32),
            pltpu.VMEM((1024, 256), F32),
            pltpu.VMEM((2, 4, 256, 256), F32),
            pltpu.VMEM((3, 4, 512, 256), i16),
            pltpu.VMEM((3, 4, 512, 256), i16),
            pltpu.VMEM((3, 3, 8, 256), F32),
            pltpu.VMEM((3, 3, 8, 256), F32),
            pltpu.VMEM((4, 512, BLK), i16),
            pltpu.VMEM((4, 512, BLK), i16),
            pltpu.VMEM((3, 8, BLK), F32),
            pltpu.VMEM((3, 8, BLK), F32),
            pltpu.VMEM((4, 512, 512), BF),
            pltpu.VMEM((1024, 2048), BF),
            pltpu.VMEM((2, 2, 4, BLK, 256), i16),
            pltpu.VMEM((2, 2, 4, BLK, 256), i16),
            pltpu.VMEM((2, 2, 4, 8, 256), F32),
            pltpu.VMEM((2, 2, 4, 8, 256), F32),
            pltpu.VMEM((512, 512), BF),
            dma((3, 4)), dma((3, 4)), dma((3,)), dma((3,)), dma((8,)), dma((8,)),
            dma((2, 4, 4)), dma((2, 4, 4)), dma((7,)), dma((7,)), dma((2, 3, 3)), dma((2, 3, 3)),
            dma((2, 3)), dma((2, 3)), dma((3, 3)), dma((3, 3)), dma((2, 2, 2, 4)), dma((2, 2, 2, 4)), dma((1,)),
        ],
        compiler_params=pltpu.CompilerParams(
            collective_id=0, has_side_effects=True, vmem_limit_bytes=56 << 20
        ),
        cost_estimate=pl.CostEstimate(
            flops=10_737_418_240, bytes_accessed=4 << 20, transcendentals=0
        ),
        name="selected_inversion",
    )(block_counts, panel, anc_inverse)
    return pl.pallas_call(
        finish,
        out_shape=(
            jax.ShapeDtypeStruct((512, 512), BF),
            jax.ShapeDtypeStruct((BLK, 512), F32),
        ),
        in_specs=[vmem()] * 3,
        out_specs=(vmem(), vmem()),
        name="diagonal_update",
    )(off, total, diag_inverse)


def solution(mesh):
    return jax.shard_map(
        per_device,
        mesh=mesh,
        in_specs=(P("prow", "pcol"), P("prow", "pcol"), P("prow", "pcol"), P()),
        out_specs=(P("prow", "pcol"), P("prow", "pcol")),
        check_vma=False,
    )
```
